32 devices in a mesh: seq: 8 (over y, x, core), head: 4 (over z).
Axes of the slice: x: 2, y: 2, z: 4, core: 2. Of those that a mesh axis runs over, the one named last changes fastest.
Arguments:
- hidden_states: bfloat16 [4, 4096, 768], P(None, 'seq'), may hold values from -6 to 6
- segment_ids: int32 [4, 4096], replicated, may hold values from 0 to 2, as said below
- norm_gain: float32 [768], replicated, may hold values from 0.5 to 1.5
- gate_weight: bfloat16 [768, 1536], P(None, 'head'), may hold values from -0.21875 to 0.21875
- value_weight: bfloat16 [768, 1536], P(None, 'head'), may hold values from -0.21875 to 0.21875
- state_weight: bfloat16 [768, 256], replicated, may hold values from -0.21875 to 0.21875
- step_weight: bfloat16 [768, 24], P(None, 'head'), may hold values from -0.21875 to 0.21875
- kernel_value: float32 [4, 1536], P(None, 'head'), may hold values from -0.6 to 0.6
- kernel_state: float32 [4, 256], replicated, may hold values from -0.6 to 0.6
- bias_value: float32 [1536], P('head'), may hold values from -0.5 to 0.5
- bias_state: float32 [256], replicated, may hold values from -0.5 to 0.5
- step_bias: float32 [24], P('head'), may hold values from -3 to 0
- decay_log: float32 [24], P('head'), may hold values from -10.8 to -0.7
- skip_gain: float32 [24], P('head'), may hold values from 0.5 to 1.5
- inner_gain: float32 [1536], P('head'), may hold values from 0.5 to 1.5
- output_weight: bfloat16 [1536, 768], P('head'), may hold values from -0.15625 to 0.15625
- cotangent: bfloat16 [4, 4096, 768], P(None, 'seq'), may hold values from -6 to 6
Outputs:
- block_output: bfloat16 [4, 4096, 768], P(None, 'seq')
- input_gradient: float32 [4, 4096, 768], P(None, 'seq')
- grad_norm_gain: float32 [768], replicated
- grad_gate_weight: float32 [768, 1536], P(None, 'head')
- grad_value_weight: float32 [768, 1536], P(None, 'head')
- grad_state_weight: float32 [768, 256], replicated
- grad_step_weight: float32 [768, 24], P(None, 'head')
- grad_kernel_value: float32 [4, 1536], P(None, 'head')
- grad_kernel_state: float32 [4, 256], replicated
- grad_bias_value: float32 [1536], P('head')
- grad_bias_state: float32 [256], replicated
- grad_step_bias: float32 [24], P('head')
- grad_decay_log: float32 [24], P('head')
- grad_skip_gain: float32 [24], P('head')
- grad_inner_gain: float32 [1536], P('head')
- grad_output_weight: float32 [1536, 768], P('head')
The draws below stay inside these ranges and needn't reach their ends.
Inputs may be any that keep to these rules, and one draw needn't show every extreme that they name: `segment_ids`: in every row the ids never fall and take 0, 1, 2 in this order: 0 covers the first 1 to 255 tokens, 2 the last 1 to 255, and 1 all the others.
All inputs are finite; a program needn't handle non-finite values.
Results may differ from the reference program's by a relative error of at most 0.015.
The reference program's roundings to bfloat16 on the way count: a program that leaves them out, or rounds other values in their place, can miss the bound.
Values may be sent and summed in bfloat16 or wider, within the bound.
No kernel may reach another device: no remote copies, remote signals or barrier semaphores. Data moves between devices by JAX's collectives and lax.ppermute only.
A program may use at most 192 MiB of HBM per device.

```python
import jax
import jax.numpy as jnp
from jax import lax

D = 768
HEADS = 24
HEADDIM = 64
STATE = 128
CONV = 4
BLOCK = 256
BATCH = 4
ROW_DEV = 512
INNER = 1536
TOKENS = 4096


def draw_segment_ids(key, part):
    key = jax.random.fold_in(key, 11)
    first_key, second_key = jax.random.split(key)
    front = jax.random.randint(first_key, (BATCH, 1), 1, ROW_DEV // 2, dtype=jnp.int32)
    tail_length = jax.random.randint(second_key, (BATCH, 1), 1, ROW_DEV // 2, dtype=jnp.int32)
    positions = jnp.arange(TOKENS, dtype=jnp.int32)[None, :]
    return (positions >= front).astype(jnp.int32) + (positions >= TOKENS - tail_length).astype(jnp.int32)


def block_scale(own_key, shape, shards, smallest, high):
    def one(position, shards_of):
        steps = jax.random.uniform(jax.random.fold_in(jax.random.fold_in(own_key, 6), position), (shards_of,), jnp.float32, smallest / len(shards), high / len(shards))
        return jnp.repeat(jnp.exp(steps), shape[position] // shards_of).reshape((-1,) + (1,) * (len(shape) - position - 1))

    level = one(*shards[0])
    for cut in shards[1:]:
        level = level * one(*cut)
    return level


def gaussian(stream_key, shape, deviation, limit, cuts=(), held_as=jnp.bfloat16):
    values = jax.random.normal(stream_key, shape, jnp.float32) * deviation
    if len(cuts) > 0:
        values = block_scale(stream_key, shape, cuts, -0.22, 0.18) * values
    return jnp.clip(values, min=-limit, max=limit).astype(held_as)


def setup_inputs(seed: int = 0) -> dict:
    splits = jax.random.split(jax.random.key(seed), 18)
    hidden_states = gaussian(splits[0], (BATCH, TOKENS, D), 1.0, 6.0, ((1, 8),))
    segment_ids = draw_segment_ids(jax.random.fold_in(splits[17], 71), 0)
    norm_gain = jnp.clip(1.0 + 0.1 * jax.random.normal(splits[2], (D,), jnp.float32), 0.5, 1.5)
    gate_weight = gaussian(splits[3], (D, INNER), D ** -0.5, 0.21875, ((1, 4),))
    value_weight = gaussian(splits[4], (D, INNER), D ** -0.5, 0.21875, ((1, 4),))
    state_weight = gaussian(splits[5], (D, 2 * STATE), D ** -0.5, 0.21875)
    step_weight = gaussian(splits[6], (D, HEADS), D ** -0.5, 0.21875, ((1, 4),))
    kernel_value = jnp.clip(jax.random.uniform(splits[7], (CONV, INNER), jnp.float32, -0.6, 0.6) * block_scale(splits[7], (CONV, INNER), ((1, 4),), -0.4, 0.0), -0.6, 0.6)
    kernel_state = jnp.clip(jax.random.uniform(splits[8], (CONV, 2 * STATE), jnp.float32, -0.6, 0.6), -0.6, 0.6)
    bias_value = jnp.clip(jax.random.uniform(splits[9], (INNER,), jnp.float32, -0.5, 0.5) * block_scale(splits[9], (INNER,), ((0, 4),), -0.4, 0.0), -0.5, 0.5)
    bias_state = jnp.clip(jax.random.uniform(splits[10], (2 * STATE,), jnp.float32, -0.5, 0.5), -0.5, 0.5)
    step_bias = jnp.clip(-3.0 + 3.0 * jax.random.uniform(splits[11], (HEADS,), jnp.float32) ** block_scale(splits[11], (HEADS,), ((0, 4),), -0.2, 0.2), -3.0, 0.0)
    decay_log = jnp.clip(-10.8 + 10.1 * jax.random.uniform(splits[12], (HEADS,), jnp.float32) ** block_scale(splits[12], (HEADS,), ((0, 4),), -0.2, 0.2), -10.8, -0.7)
    skip_gain = jnp.clip(0.5 + 1.0 * jax.random.uniform(splits[13], (HEADS,), jnp.float32) ** block_scale(splits[13], (HEADS,), ((0, 4),), -0.2, 0.2), 0.5, 1.5)
    inner_gain = jnp.clip(1.0 + 0.1 * jax.random.normal(splits[14], (INNER,), jnp.float32), 0.5, 1.5)
    output_weight = gaussian(splits[15], (INNER, D), INNER ** -0.5, 0.15625, ((0, 4),))
    cotangent = gaussian(splits[16], (BATCH, TOKENS, D), 1.0, 6.0, ((1, 8),))
    return dict(hidden_states=hidden_states, segment_ids=segment_ids, norm_gain=norm_gain, gate_weight=gate_weight, value_weight=value_weight, state_weight=state_weight, step_weight=step_weight, kernel_value=kernel_value, kernel_state=kernel_state, bias_value=bias_value, bias_state=bias_state, step_bias=step_bias, decay_log=decay_log, skip_gain=skip_gain, inner_gain=inner_gain, output_weight=output_weight, cotangent=cotangent)


EPSILON = 1e-05
HIGHEST = lax.Precision.HIGHEST

@jax.custom_vjp
def low(v):
    return lax.optimization_barrier(v.astype(jnp.bfloat16)).astype(jnp.float32)

@jax.custom_vjp
def low_back(v):
    return v

def low_keep(v):
    return (low(v), None)

def low_pass(kept, grad):
    return (grad,)

def back_keep(v):
    return (v, None)

def back_low(kept, grad):
    return (low(grad),)
low.defvjp(low_keep, low_pass)
low_back.defvjp(back_keep, back_low)

def silu_of(values):
    return values * jax.nn.sigmoid(values)

def block_step(carried_pair, pieces):
    carried, last_segment = carried_pair
    value_block, write_block, read_block, decay_block, step_block, segment_block = pieces
    running = jnp.cumsum(decay_block, axis=0)
    positions = jnp.arange(BLOCK)
    linked = (segment_block[:, None] == segment_block[None, :]) & (positions[:, None] >= positions[None, :])
    linked_float = linked.astype(jnp.float32)[:, :, None]
    spread = jnp.where(linked[:, :, None], running[:, None, :] - running[None, :, :], 0.0)
    scores = jnp.dot(read_block, write_block.T, precision=HIGHEST)
    weights = scores[:, :, None] * jnp.exp(spread) * linked_float * step_block[None, :, :]
    output = jnp.einsum('tsh,shp->thp', weights, value_block, precision=HIGHEST)
    joined = (segment_block == last_segment).astype(jnp.float32)[:, None] * jnp.exp(running)
    output = output + joined[:, :, None] * jnp.einsum('tn,hpn->thp', read_block, carried, precision=HIGHEST)
    final_segment = segment_block[BLOCK - 1]
    toward = (segment_block == final_segment).astype(jnp.float32)[:, None] * jnp.exp(running[BLOCK - 1][None, :] - running) * step_block
    keep_rate = (final_segment == last_segment).astype(jnp.float32) * jnp.exp(running[BLOCK - 1])
    carried = keep_rate[:, None, None] * carried + jnp.einsum('sh,shp,sn->hpn', toward, value_block, write_block, precision=HIGHEST)
    return ((carried, final_segment), output)

def scan_row(values, writers, readers, log_decay, step_size, segments, initial_segment):
    length, head_count = log_decay.shape
    block_count = length // BLOCK
    pieces = (values.reshape(block_count, BLOCK, head_count, HEADDIM), writers.reshape(block_count, BLOCK, STATE), readers.reshape(block_count, BLOCK, STATE), log_decay.reshape(block_count, BLOCK, head_count), step_size.reshape(block_count, BLOCK, head_count), segments.reshape(block_count, BLOCK))
    initial = (jnp.zeros((head_count, HEADDIM, STATE), jnp.float32), initial_segment)
    final_pair, outputs = lax.scan(jax.checkpoint(block_step), initial, pieces)
    return outputs.reshape(length, head_count, HEADDIM)

def forward_row(params, hidden, segments):
    norm_gain, gate_weight, value_weight, state_weight, step_weight, kernel_value, kernel_state, bias_value, bias_state, step_bias, decay_log, skip_gain, inner_gain, output_weight = params
    length = hidden.shape[0]
    norm_scale = lax.rsqrt(lax.optimization_barrier(jnp.mean(hidden * hidden, axis=1, keepdims=True)) + EPSILON)
    normed = low(hidden * norm_scale * norm_gain)
    gate_pre = low_back(jnp.dot(normed, gate_weight, precision=HIGHEST))
    inner_values = low_back(jnp.dot(normed, value_weight, precision=HIGHEST))
    inner_states = low_back(jnp.dot(normed, state_weight, precision=HIGHEST))
    step_raw = low_back(jnp.dot(normed, step_weight, precision=HIGHEST))
    mixed_in = low(jnp.concatenate([inner_values, inner_states], axis=1))
    kernel = jnp.concatenate([kernel_value, kernel_state], axis=1)
    shift_bias = jnp.concatenate([bias_value, bias_state])
    padded = jnp.concatenate([jnp.zeros((CONV - 1, mixed_in.shape[1]), jnp.float32), mixed_in], axis=0)
    padded_segments = jnp.concatenate([jnp.full((CONV - 1,), -1, jnp.int32), segments])
    summed = shift_bias[None, :]
    for offset in range(CONV):
        same_segment = (padded_segments[offset:offset + length] == segments).astype(jnp.float32)[:, None]
        summed = summed + kernel[offset] * padded[offset:offset + length] * same_segment
    activated = low(silu_of(summed))
    values = activated[:, :INNER].reshape(length, HEADS, HEADDIM)
    writers = activated[:, INNER:INNER + STATE]
    readers = activated[:, INNER + STATE:]
    step_size = jax.nn.softplus(step_raw + step_bias)
    log_decay = -step_size * jnp.exp(decay_log)
    scanned = scan_row(values, writers, readers, log_decay, step_size, segments, jnp.array(-1, jnp.int32))
    scanned = (scanned + skip_gain[None, :, None] * values).reshape(length, INNER)
    gated = scanned * silu_of(gate_pre)
    gate_scale = lax.rsqrt(lax.optimization_barrier(jnp.mean(gated * gated, axis=1, keepdims=True)) + EPSILON)
    out_in = low(gated * gate_scale * inner_gain)
    return hidden + jnp.dot(out_in, output_weight, precision=HIGHEST)

def reference(hidden_states, segment_ids, norm_gain, gate_weight, value_weight, state_weight, step_weight, kernel_value, kernel_state, bias_value, bias_state, step_bias, decay_log, skip_gain, inner_gain, output_weight, cotangent):
    params = (norm_gain.astype(jnp.float32), gate_weight.astype(jnp.float32), value_weight.astype(jnp.float32), state_weight.astype(jnp.float32), step_weight.astype(jnp.float32), kernel_value.astype(jnp.float32), kernel_state.astype(jnp.float32), bias_value.astype(jnp.float32), bias_state.astype(jnp.float32), step_bias.astype(jnp.float32), decay_log.astype(jnp.float32), skip_gain.astype(jnp.float32), inner_gain.astype(jnp.float32), output_weight.astype(jnp.float32))

    def one_row(totals, pieces):
        hidden_row, segment_row, cotangent_row = pieces

        def forward_of(weights, hidden):
            return forward_row(weights, hidden, segment_row)
        result, pullback = jax.vjp(forward_of, params, hidden_row.astype(jnp.float32))
        weight_grads, input_grad = pullback(cotangent_row.astype(jnp.float32))
        totals = jax.tree.map(jnp.add, totals, weight_grads)
        return (totals, (result.astype(jnp.bfloat16), input_grad))
    zero_grads = jax.tree.map(jnp.zeros_like, params)
    totals, (block_output, input_gradient) = lax.scan(one_row, zero_grads, (hidden_states, segment_ids, cotangent))
    return (block_output, input_gradient, totals[0], totals[1], totals[2], totals[3], totals[4], totals[5], totals[6], totals[7], totals[8], totals[9], totals[10], totals[11], totals[12], totals[13])
```

```python
import jax
import jax.numpy as jnp
from jax import lax
from jax.experimental import pallas as pl
from jax.experimental.pallas import tpu as pltpu
from jax.sharding import PartitionSpec as P

HEADDIM = 64
STATE = 128
EPSILON = 1e-05
HIGHEST = lax.Precision.HIGHEST
LANES = 128
HALO = 16
TILE = 256
BF16 = jnp.bfloat16
F32 = jnp.float32
VMEM_LIMIT = 56 * 1024 * 1024


def bits_of(count):
    return count.bit_length() - 1


def swap(value, axis, bit):
    count = lax.axis_size(axis)
    return lax.ppermute(value, axis, [(i, i ^ (1 << bit)) for i in range(count)])


def bit_of(axis, bit):
    return (lax.axis_index(axis) >> bit) & 1


def joined(mine, other, upper):
    return jnp.where(
        upper == 1,
        jnp.concatenate([other, mine], axis=0),
        jnp.concatenate([mine, other], axis=0),
    )


def seq_rank():
    bits = bits_of(lax.axis_size("seq"))
    return sum(bit_of("seq", b) << (bits - 1 - b) for b in range(bits))


def gather_head(value):
    for b in range(bits_of(lax.axis_size("head"))):
        value = joined(value, swap(value, "head", b), bit_of("head", b))
    return value


def gather_seq(value):
    for b in reversed(range(bits_of(lax.axis_size("seq")))):
        value = joined(value, swap(value, "seq", b), bit_of("seq", b))
    return value


def gather_weight(weight):
    seq_count, head_count = lax.axis_size("seq"), lax.axis_size("head")
    part = weight.shape[0] // seq_count
    own = lax.dynamic_slice_in_dim(weight, seq_rank() * part, part, 0)
    whole = gather_seq(gather_head(own[None]))
    return whole.reshape(seq_count, head_count, part, weight.shape[1])


def halve(value, axis, bit):
    value = value.reshape((2, value.shape[0] // 2) + value.shape[1:])
    upper = bit_of(axis, bit)
    keep = lax.dynamic_index_in_dim(value, upper, 0, keepdims=False)
    send = lax.dynamic_index_in_dim(value, 1 - upper, 0, keepdims=False)
    got = swap(send, axis, bit)
    return (keep.astype(F32) + got.astype(F32)).astype(value.dtype)


def scatter_seq(value):
    for b in range(bits_of(lax.axis_size("seq"))):
        value = halve(value, "seq", b)
    return value


def reduce_weight(grad):
    seq_count, head_count, part, width = grad.shape
    grad = scatter_seq(grad.reshape(seq_count * head_count, part, width))
    for b in reversed(range(bits_of(head_count))):
        grad = halve(grad, "head", b)
    return gather_seq(grad).reshape(seq_count * part, width)


def reduce_all(value):
    value = scatter_seq(value)
    for b in range(bits_of(lax.axis_size("head"))):
        value = (value.astype(F32) + swap(value, "head", b).astype(F32)).astype(value.dtype)
    return gather_seq(value)


def chunk_permute(value, rows, target):
    seq_count, head_count = lax.axis_size("seq"), lax.axis_size("head")
    parts = head_count // rows
    pairs = []
    for s in range(seq_count):
        for h in range(head_count):
            goal = target(s * parts + h % parts)
            if 0 <= goal < seq_count * parts:
                place = (goal // parts) * head_count + (h // parts) * parts + goal % parts
                pairs.append((s * head_count + h, place))
    return lax.ppermute(value, ("seq", "head"), pairs)


def carried(rate, state, rows, chunk, reverse):
    count = lax.axis_size("seq") * (lax.axis_size("head") // rows)
    before = jnp.zeros_like(state)
    before_rate = jnp.ones_like(rate)
    for b in range(bits_of(count)):
        got = chunk_permute(state.astype(BF16), rows, lambda c: c ^ (1 << b)).astype(F32)
        got_rate = chunk_permute(rate, rows, lambda c: c ^ (1 << b))
        after = ((chunk >> b) & 1) == (0 if reverse else 1)
        before = jnp.where(after, before_rate[:, None] * got + before, before)
        before_rate = jnp.where(after, before_rate * got_rate, before_rate)
        if b < bits_of(count) - 1:
            state = jnp.where(
                after, rate[:, None] * got + state, got_rate[:, None] * state + got
            )
            rate = rate * got_rate
    return before


def contract(a, b, dims):
    return lax.dot_general(a, b, ((dims[0], dims[1]), ((), ())), preferred_element_type=F32)


def taps_of(padded, masks):
    taps = []
    for k in range(4):
        moved = padded if k == 3 else pltpu.roll(padded, 3 - k, 0)
        tap = moved[HALO:]
        taps.append(tap if k == 3 else tap * masks[:, k : k + 1])
    return taps


def summed_of(taps, kernel, bias):
    summed = bias
    for k in range(4):
        summed = summed + kernel[k : k + 1, :] * taps[k]
    return summed


def linked_of(seg_col, seg_row):
    length = seg_col.shape[0]
    row = lax.broadcasted_iota(jnp.int32, (length, length), 0)
    col = lax.broadcasted_iota(jnp.int32, (length, length), 1)
    return jnp.where((row >= col) & (seg_col == seg_row), 1.0, 0.0)


def blocks_of(length):
    count = length // TILE
    return [(t, s) for t in range(count) for s in range(t + 1)]


def cut(index):
    return slice(index * TILE, (index + 1) * TILE)


def scan_kernel(
    mixed_ref,
    states_ref,
    kernel_ref,
    bias_ref,
    kernel_state_ref,
    bias_state_ref,
    masks_ref,
    seg_col_ref,
    seg_row_ref,
    step_ref,
    decay_ref,
    x_ref,
    open_ref,
    end_ref,
    run_ref,
    size_ref,
    writers_ref,
    readers_ref,
    turned_ref,
    scores,
    run_all,
    size_all,
):
    pair = pl.program_id(0)
    length = x_ref.shape[0]
    pairs = run_all.shape[0]
    low = lax.broadcasted_iota(jnp.int32, (1, LANES), 1) < HEADDIM
    masks = masks_ref[...]

    @pl.when(pair == 0)
    def _():
        taps = taps_of(states_ref[...].astype(F32), masks)
        summed = summed_of(taps, kernel_state_ref[...], bias_state_ref[...])
        active = (summed * jax.nn.sigmoid(summed)).astype(BF16)
        writers = active[:, :STATE]
        readers = active[:, STATE:]
        writers_ref[...] = writers
        readers_ref[...] = readers
        linked = linked_of(seg_col_ref[...], seg_row_ref[...])
        scores[...] = contract(readers, writers, ((1,), (1,))) * linked
        row = lax.broadcasted_iota(jnp.int32, (length, length), 0)
        col = lax.broadcasted_iota(jnp.int32, (length, length), 1)
        lower = jnp.where(row >= col, 1.0, 0.0)
        run = jnp.dot(lower, decay_ref[...], precision=HIGHEST, preferred_element_type=F32)
        turned_ref[...] = run.T
        size = step_ref[...]
        for i in range(pairs):
            a, b = 2 * i, 2 * i + 1
            run_all[i] = jnp.where(low, run[:, a : a + 1], run[:, b : b + 1])
            size_all[i] = jnp.where(low, size[:, a : a + 1], size[:, b : b + 1])

    run = run_all[pair]
    size = size_all[pair]
    run_ref[...] = run
    size_ref[...] = size
    taps = taps_of(mixed_ref[...].astype(F32), masks)
    summed = summed_of(taps, kernel_ref[...], bias_ref[...])
    x = (summed * jax.nn.sigmoid(summed)).astype(BF16)
    x_ref[...] = x
    sized = x.astype(F32) * size
    sized_low = sized.astype(BF16)
    zero = jnp.zeros((), BF16)
    halves = (jnp.where(low, sized_low, zero), jnp.where(low, zero, sized_low))
    totals = [None] * (length // TILE)
    for t, s in blocks_of(length):
        score = scores[cut(t), cut(s)]
        for j in range(2):
            row = turned_ref[pl.ds(2 * pair + j, 1), :][:, cut(s)]
            col = run[cut(t), j * HEADDIM : j * HEADDIM + 1]
            weight = (score * jnp.exp(jnp.minimum(col - row, 0.0))).astype(BF16)
            part = contract(weight, halves[j][cut(s)], ((1,), (0,)))
            totals[t] = part if totals[t] is None else totals[t] + part
    for t, total in enumerate(totals):
        open_ref[cut(t), :] = total
    seg_col = seg_col_ref[...]
    last = jnp.where(seg_col == seg_col[length - 1 : length, :], 1.0, 0.0)
    toward = last * jnp.exp(run[length - 1 : length, :] - run)
    end_ref[...] = contract((toward * sized).astype(BF16), writers_ref[...], ((0,), (0,)))


def gate_kernel(
    open_ref,
    x_ref,
    run_ref,
    gate_ref,
    grad_out_ref,
    hidden_ref,
    entered_ref,
    readers_ref,
    start_ref,
    weight_ref,
    gain_ref,
    skip_ref,
    total_ref,
    out_in_ref,
    block_ref,
    grad_scan_ref,
    grad_gate_ref,
    grad_read_ref,
    sums_ref,
    grad_start_ref,
):
    step = pl.program_id(0)
    inner = gain_ref.shape[1]
    gain = gain_ref[...]
    x = x_ref[...].astype(F32)
    start = start_ref[...]
    readers = readers_ref[...]
    reach = entered_ref[...] * jnp.exp(run_ref[...])
    total = open_ref[...] + reach * contract(readers, start, ((1,), (1,)))
    total_ref[...] = total
    scanned = total + skip_ref[...] * x
    gate = gate_ref[...]
    sig = jax.nn.sigmoid(gate)
    act = gate * sig
    gated = scanned * act
    scale = lax.rsqrt(jnp.sum(gated * gated, axis=1, keepdims=True) / inner + EPSILON)
    unit = gated * scale
    out_in = (unit * gain).astype(BF16)
    out_in_ref[...] = out_in
    branch = contract(out_in, weight_ref[...], ((1,), (0,)))
    block_ref[...] = (hidden_ref[...].astype(F32) + branch).astype(BF16)
    grad_out = grad_out_ref[...]
    q = grad_out * gain
    inner_product = jnp.sum(q * gated, axis=1, keepdims=True) / inner
    grad_gated = scale * q - gated * (scale * scale * scale * inner_product)
    grad_scan = grad_gated * act
    grad_scan_low = grad_scan.astype(BF16)
    grad_scan_ref[...] = grad_scan_low
    slope = sig * (1.0 + gate * (1.0 - sig))
    grad_gate_ref[...] = (grad_gated * scanned * slope).astype(BF16)
    reached = (reach * grad_scan).astype(BF16)
    grad_read_ref[...] = contract(reached, start, ((1,), (0,)))
    grad_start = contract(reached, readers, ((0,), (0,)))
    gain_sum = jnp.sum(grad_out * unit, axis=0, keepdims=True)
    skip_sum = jnp.sum(grad_scan * x, axis=0, keepdims=True)
    rows = lax.broadcasted_iota(jnp.int32, (8, inner), 0)
    sums = jnp.where(rows == 0, gain_sum, jnp.where(rows == 1, skip_sum, 0.0))

    @pl.when(step == 0)
    def _():
        sums_ref[...] = sums
        grad_start_ref[...] = grad_start

    @pl.when(step > 0)
    def _():
        sums_ref[...] += sums
        grad_start_ref[...] += grad_start


def conv_back(grad_act, padded, kernel, bias, masks):
    length, width = grad_act.shape
    taps = taps_of(padded, masks)
    summed = summed_of(taps, kernel, bias)
    sig = jax.nn.sigmoid(summed)
    grad_u = grad_act * (sig * (1.0 + summed * (1.0 - sig)))
    rows = lax.broadcasted_iota(jnp.int32, (8, width), 0)
    sums = jnp.where(rows == 4, jnp.sum(grad_u, axis=0, keepdims=True), 0.0)
    mixed = None
    nothing = jnp.zeros((HALO, width), F32)
    for k in range(4):
        sums = jnp.where(rows == k, jnp.sum(grad_u * taps[k], axis=0, keepdims=True), sums)
        back = grad_u * kernel[k : k + 1, :]
        if k < 3:
            back = back * masks[:, k : k + 1]
        back = jnp.concatenate([nothing, back], axis=0)
        if k < 3:
            back = pltpu.roll(back, length + HALO - (3 - k), 0)
        mixed = back if mixed is None else mixed + back
    return mixed, sums


def back_kernel(
    x_ref,
    mixed_ref,
    run_ref,
    size_ref,
    grad_scan_ref,
    total_ref,
    grad_end_ref,
    start_ref,
    kernel_ref,
    bias_ref,
    skip_ref,
    states_ref,
    kernel_state_ref,
    bias_state_ref,
    masks_ref,
    seg_col_ref,
    seg_row_ref,
    writers_ref,
    readers_ref,
    turned_ref,
    grad_read_ref,
    grad_mixed_ref,
    sums_ref,
    grad_states_ref,
    sums_state_ref,
    rate_ref,
    direct_ref,
    scores,
    grad_scores,
    grad_write,
    rate_sum,
    direct_sum,
):
    pair = pl.program_id(0)
    length = x_ref.shape[0]
    low = lax.broadcasted_iota(jnp.int32, (1, LANES), 1) < HEADDIM
    lane = lax.broadcasted_iota(jnp.int32, (1, LANES), 1)
    masks = masks_ref[...]
    writers = writers_ref[...]
    readers = readers_ref[...]
    seg_col = seg_col_ref[...]

    @pl.when(pair == 0)
    def _():
        linked = linked_of(seg_col, seg_row_ref[...])
        scores[...] = contract(readers, writers, ((1,), (1,))) * linked
        grad_scores[...] = jnp.zeros_like(grad_scores)
        grad_write[...] = jnp.zeros_like(grad_write)
        rate_sum[...] = jnp.zeros_like(rate_sum)
        direct_sum[...] = jnp.zeros_like(direct_sum)

    run = run_ref[...]
    size = size_ref[...]
    x = x_ref[...].astype(F32)
    sized = x * size
    sized_low = sized.astype(BF16)
    grad_scan = grad_scan_ref[...]
    zero = jnp.zeros((), BF16)
    halves = (jnp.where(low, grad_scan, zero), jnp.where(low, zero, grad_scan))
    inner = [None] * (length // TILE)
    for t, s in blocks_of(length):
        score = scores[cut(t), cut(s)]
        grad_score = grad_scores[cut(t), cut(s)]
        for j in range(2):
            row = turned_ref[pl.ds(2 * pair + j, 1), :][:, cut(s)]
            col = run[cut(t), j * HEADDIM : j * HEADDIM + 1]
            decay = jnp.exp(jnp.minimum(col - row, 0.0))
            weight = (score * decay).astype(BF16)
            grad_weight = contract(halves[j][cut(t)], sized_low[cut(s)], ((1,), (1,)))
            grad_score = grad_score + grad_weight * decay
            part = contract(weight, halves[j][cut(t)], ((0,), (0,)))
            inner[s] = part if inner[s] is None else inner[s] + part
        grad_scores[cut(t), cut(s)] = grad_score
    inner = inner[0] if len(inner) == 1 else jnp.concatenate(inner, axis=0)
    last = jnp.where(seg_col == seg_col[length - 1 : length, :], 1.0, 0.0)
    toward = last * jnp.exp(run[length - 1 : length, :] - run)
    grad_end = grad_end_ref[...]
    outer = toward * contract(writers, grad_end.astype(BF16), ((1,), (1,)))
    grad_write[...] += contract(
        (toward * sized).astype(BF16), grad_end.astype(BF16), ((1,), (0,))
    )
    grad_sized = inner + outer
    grad_scan = grad_scan.astype(F32)
    sized_low = sized_low.astype(F32)
    change = grad_scan * total_ref[...] - sized_low * grad_sized
    straight = x * grad_sized
    for j in range(2):
        side = low if j == 0 else jnp.logical_not(low)
        here = lane == 2 * pair + j
        one = jnp.sum(jnp.where(side, change, 0.0), axis=1, keepdims=True)
        rate_sum[...] += jnp.where(here, one, 0.0)
        two = jnp.sum(jnp.where(side, straight, 0.0), axis=1, keepdims=True)
        direct_sum[...] += jnp.where(here, two, 0.0)
    grad_x = size * grad_sized + skip_ref[...] * grad_scan
    grad_mixed, sums = conv_back(
        grad_x, mixed_ref[...].astype(F32), kernel_ref[...], bias_ref[...], masks
    )
    grad_mixed_ref[...] = grad_mixed
    rows = lax.broadcasted_iota(jnp.int32, (8, LANES), 0)
    outer_sum = jnp.sum(sized_low * outer, axis=0, keepdims=True)
    kept = start_ref[...].astype(F32) * grad_end
    kept_low = jnp.sum(kept[:HEADDIM], axis=0, keepdims=True)
    kept_high = jnp.sum(kept[HEADDIM:], axis=0, keepdims=True)
    sums = jnp.where(rows == 5, outer_sum, sums)
    sums = jnp.where(rows == 6, kept_low, jnp.where(rows == 7, kept_high, sums))
    sums_ref[...] = sums

    @pl.when(pair == pl.num_programs(0) - 1)
    def _():
        linked = linked_of(seg_col, seg_row_ref[...])
        grad_score = (grad_scores[...] * linked).astype(BF16)
        grad_readers = contract(grad_score, writers, ((1,), (0,))) + grad_read_ref[...]
        grad_writers = contract(grad_score, readers, ((0,), (0,))) + grad_write[...]
        grad_act = jnp.concatenate([grad_writers, grad_readers], axis=1)
        grad_states, state_sums = conv_back(
            grad_act,
            states_ref[...].astype(F32),
            kernel_state_ref[...],
            bias_state_ref[...],
            masks,
        )
        grad_states_ref[...] = grad_states
        sums_state_ref[...] = state_sums
        row = lax.broadcasted_iota(jnp.int32, (length, length), 0)
        col = lax.broadcasted_iota(jnp.int32, (length, length), 1)
        upper = jnp.where(col >= row, 1.0, 0.0)
        rate_ref[...] = jnp.dot(
            upper, rate_sum[...], precision=HIGHEST, preferred_element_type=F32
        )
        direct_ref[...] = direct_sum[...]


def whole_spec(shape):
    return pl.BlockSpec(shape, lambda i: (0,) * len(shape))


def columns_spec(rows):
    return pl.BlockSpec((rows, LANES), lambda i: (0, i))


def rows_spec(rows, width):
    return pl.BlockSpec((rows, width), lambda i: (i, 0))


def run_scan(mixed, states, kernel, bias, kernel_state, bias_state, masks, seg_col, seg_row, step, decay):
    length = mixed.shape[0] - HALO
    inner = mixed.shape[1]
    pairs = inner // LANES
    wide = 2 * STATE
    return pl.pallas_call(
        scan_kernel,
        grid=(pairs,),
        in_specs=[
            columns_spec(length + HALO),
            whole_spec((length + HALO, wide)),
            columns_spec(4),
            columns_spec(1),
            whole_spec((4, wide)),
            whole_spec((1, wide)),
            whole_spec((length, 4)),
            whole_spec((length, 1)),
            whole_spec((1, length)),
            whole_spec((length, LANES)),
            whole_spec((length, LANES)),
        ],
        out_specs=[
            columns_spec(length),
            columns_spec(length),
            rows_spec(LANES, STATE),
            columns_spec(length),
            columns_spec(length),
            whole_spec((length, STATE)),
            whole_spec((length, STATE)),
            whole_spec((LANES, length)),
        ],
        out_shape=[
            jax.ShapeDtypeStruct((length, inner), BF16),
            jax.ShapeDtypeStruct((length, inner), F32),
            jax.ShapeDtypeStruct((inner, STATE), F32),
            jax.ShapeDtypeStruct((length, inner), F32),
            jax.ShapeDtypeStruct((length, inner), F32),
            jax.ShapeDtypeStruct((length, STATE), BF16),
            jax.ShapeDtypeStruct((length, STATE), BF16),
            jax.ShapeDtypeStruct((LANES, length), F32),
        ],
        scratch_shapes=[
            pltpu.VMEM((length, length), F32),
            pltpu.VMEM((pairs, length, LANES), F32),
            pltpu.VMEM((pairs, length, LANES), F32),
        ],
        compiler_params=pltpu.CompilerParams(vmem_limit_bytes=VMEM_LIMIT),
        name="scan_forward",
    )(mixed, states, kernel, bias, kernel_state, bias_state, masks, seg_col, seg_row, step, decay)


def run_gate(opened, x, run, gate, grad_out, hidden, entered, readers, start, weight, gain, skip):
    length, inner = x.shape
    width = hidden.shape[1]
    tile = 128
    return pl.pallas_call(
        gate_kernel,
        grid=(length // tile,),
        in_specs=[
            rows_spec(tile, inner),
            rows_spec(tile, inner),
            rows_spec(tile, inner),
            rows_spec(tile, inner),
            rows_spec(tile, inner),
            rows_spec(tile, width),
            rows_spec(tile, 1),
            rows_spec(tile, STATE),
            whole_spec((inner, STATE)),
            whole_spec((inner, width)),
            whole_spec((1, inner)),
            whole_spec((1, inner)),
        ],
        out_specs=[
            rows_spec(tile, inner),
            rows_spec(tile, inner),
            rows_spec(tile, width),
            rows_spec(tile, inner),
            rows_spec(tile, inner),
            rows_spec(tile, STATE),
            whole_spec((8, inner)),
            whole_spec((inner, STATE)),
        ],
        out_shape=[
            jax.ShapeDtypeStruct((length, inner), F32),
            jax.ShapeDtypeStruct((length, inner), BF16),
            jax.ShapeDtypeStruct((length, width), BF16),
            jax.ShapeDtypeStruct((length, inner), BF16),
            jax.ShapeDtypeStruct((length, inner), BF16),
            jax.ShapeDtypeStruct((length, STATE), F32),
            jax.ShapeDtypeStruct((8, inner), F32),
            jax.ShapeDtypeStruct((inner, STATE), F32),
        ],
        compiler_params=pltpu.CompilerParams(vmem_limit_bytes=VMEM_LIMIT),
        name="gate_both",
    )(opened, x, run, gate, grad_out, hidden, entered, readers, start, weight, gain, skip)


def run_back(
    x, mixed, run, size, grad_scan, total, grad_end, start, kernel, bias, skip,
    states, kernel_state, bias_state, masks, seg_col, seg_row, writers, readers, turned, grad_read,
):
    length, inner = x.shape
    wide = 2 * STATE
    return pl.pallas_call(
        back_kernel,
        grid=(inner // LANES,),
        in_specs=[
            columns_spec(length),
            columns_spec(length + HALO),
            columns_spec(length),
            columns_spec(length),
            columns_spec(length),
            columns_spec(length),
            rows_spec(LANES, STATE),
            rows_spec(LANES, STATE),
            columns_spec(4),
            columns_spec(1),
            columns_spec(1),
            whole_spec((length + HALO, wide)),
            whole_spec((4, wide)),
            whole_spec((1, wide)),
            whole_spec((length, 4)),
            whole_spec((length, 1)),
            whole_spec((1, length)),
            whole_spec((length, STATE)),
            whole_spec((length, STATE)),
            whole_spec((LANES, length)),
            whole_spec((length, STATE)),
        ],
        out_specs=[
            columns_spec(length + HALO),
            columns_spec(8),
            whole_spec((length + HALO, wide)),
            whole_spec((8, wide)),
            whole_spec((length, LANES)),
            whole_spec((length, LANES)),
        ],
        out_shape=[
            jax.ShapeDtypeStruct((length + HALO, inner), F32),
            jax.ShapeDtypeStruct((8, inner), F32),
            jax.ShapeDtypeStruct((length + HALO, wide), F32),
            jax.ShapeDtypeStruct((8, wide), F32),
            jax.ShapeDtypeStruct((length, LANES), F32),
            jax.ShapeDtypeStruct((length, LANES), F32),
        ],
        scratch_shapes=[
            pltpu.VMEM((length, length), F32),
            pltpu.VMEM((length, length), F32),
            pltpu.VMEM((length, STATE), F32),
            pltpu.VMEM((length, LANES), F32),
            pltpu.VMEM((length, LANES), F32),
        ],
        compiler_params=pltpu.CompilerParams(vmem_limit_bytes=VMEM_LIMIT),
        name="scan_backward",
    )(
        x, mixed, run, size, grad_scan, total, grad_end, start, kernel, bias, skip,
        states, kernel_state, bias_state, masks, seg_col, seg_row, writers, readers, turned, grad_read,
    )


def dot(a, b):
    return jnp.dot(a, b, preferred_element_type=F32)


def dot_rows(a, b):
    return lax.dot_general(a, b, (((0,), (0,)), ((), ())), preferred_element_type=F32)


def dot_turned(a, b):
    return lax.dot_general(a, b, (((1,), (1,)), ((), ())), preferred_element_type=F32)


def to_columns(gathered):
    seq_count, head_count, part, width = gathered.shape
    return gathered.transpose(0, 2, 1, 3).reshape(seq_count * part, head_count * width)


def from_columns(grad, head_count):
    seq_count = lax.axis_size("seq")
    rows, columns = grad.shape
    split = grad.astype(BF16).reshape(
        seq_count, rows // seq_count, head_count, columns // head_count
    )
    return split.transpose(0, 2, 1, 3)


def to_rows(gathered):
    seq_count, head_count, part, width = gathered.shape
    return gathered.transpose(1, 0, 2, 3).reshape(seq_count * head_count * part, width)


def from_rows(grad, head_count):
    seq_count = lax.axis_size("seq")
    rows, columns = grad.shape
    split = grad.astype(BF16).reshape(
        head_count, seq_count, rows // (seq_count * head_count), columns
    )
    return split.transpose(1, 0, 2, 3)


def pad_lanes(value):
    return jnp.pad(value, ((0, 0), (0, LANES - value.shape[1])))


def shards(
    hidden_states,
    segment_ids,
    norm_gain,
    gate_weight,
    value_weight,
    state_weight,
    step_weight,
    kernel_value,
    kernel_state,
    bias_value,
    bias_state,
    step_bias,
    decay_log,
    skip_gain,
    inner_gain,
    output_weight,
    cotangent,
):
    rows, block, width = hidden_states.shape
    head_devices = lax.axis_size("head")
    parts = head_devices // rows
    length = block // parts
    seq_index, head_index = lax.axis_index("seq"), lax.axis_index("head")
    row_index, part_index = head_index // parts, head_index % parts
    chunk = seq_index * parts + part_index
    local_inner = gate_weight.shape[1]
    local_heads = step_bias.shape[0]
    inner = local_inner * head_devices
    heads = local_heads * head_devices
    taps = kernel_value.shape[0]

    value_full = to_columns(gather_weight(value_weight))
    gate_full = to_columns(gather_weight(gate_weight))
    output_full = to_rows(gather_weight(output_weight))
    step_full = gather_head(step_weight[None])
    step_full = step_full.transpose(1, 0, 2).reshape(width, heads)
    small = jnp.concatenate(
        [kernel_value.reshape(-1), bias_value, inner_gain, step_bias, decay_log, skip_gain]
    )
    small = gather_head(small[None])
    at = taps * local_inner
    kernel_full = small[:, :at].reshape(head_devices, taps, local_inner)
    kernel_full = kernel_full.transpose(1, 0, 2).reshape(taps, inner)
    bias_full = small[:, at : at + local_inner].reshape(1, inner)
    at += local_inner
    gain_full = small[:, at : at + local_inner].reshape(1, inner)
    at += local_inner
    step_bias_full = small[:, at : at + local_heads].reshape(heads)
    at += local_heads
    decay_full = jnp.exp(small[:, at : at + local_heads].reshape(heads))
    at += local_heads
    skip_full = small[:, at : at + local_heads].reshape(heads)
    skip_wide = jnp.repeat(skip_full, HEADDIM)[None]

    place = (row_index, part_index * length, 0)
    hidden_low = lax.dynamic_slice(hidden_states, place, (1, length, width))[0]
    cot = lax.dynamic_slice(cotangent, place, (1, length, width))[0]
    edge = chunk_permute(hidden_low[length - HALO :], rows, lambda c: c + 1)
    hidden_ext = jnp.concatenate([edge, hidden_low], axis=0).astype(F32)
    scale_ext = lax.rsqrt(jnp.mean(hidden_ext * hidden_ext, axis=1, keepdims=True) + EPSILON)
    normed_ext = (hidden_ext * scale_ext * norm_gain).astype(BF16)
    normed = normed_ext[HALO:]
    hidden = hidden_low.astype(F32)
    norm_scale = scale_ext[HALO:]

    seg_line = lax.dynamic_slice_in_dim(segment_ids, row_index, 1, 0)[0]
    seg_line = jnp.concatenate([jnp.full((HALO,), -1, jnp.int32), seg_line])
    window = lax.dynamic_slice_in_dim(seg_line, chunk * length, length + HALO, 0)
    segments = window[HALO:]
    before = window[HALO - 1]
    masks = jnp.stack(
        [window[HALO - 3 + k : HALO - 3 + k + length] == segments for k in range(taps)], axis=1
    ).astype(F32)
    entered = (segments == before).astype(F32)[:, None]
    seg_col = segments.astype(F32)[:, None]
    seg_row = segments.astype(F32)[None]

    mixed = dot(normed_ext, value_full).astype(BF16)
    states = dot(normed_ext, state_weight).astype(BF16)
    step_raw = dot(normed, step_full) + step_bias_full
    step_size = jax.nn.softplus(step_raw)
    log_decay = -step_size * decay_full
    passing = jnp.exp(jnp.sum(log_decay, axis=0)) * (segments[length - 1] == before).astype(F32)
    passing_wide = jnp.repeat(passing, HEADDIM)

    kernel_rows = kernel_full
    bias_state_row = bias_state[None]
    x, opened, end_state, run, size, writers, readers, turned = run_scan(
        mixed,
        states,
        kernel_rows,
        bias_full,
        kernel_state,
        bias_state_row,
        masks,
        seg_col,
        seg_row,
        pad_lanes(step_size),
        pad_lanes(log_decay),
    )
    start = carried(passing_wide, end_state, rows, chunk, False).astype(BF16)
    gate_pre = dot(normed, gate_full)
    grad_out_in = dot_turned(cot, output_full)
    total, out_in, block_rows, grad_scan, grad_gate, grad_read, gate_sums, grad_start = run_gate(
        opened,
        x,
        run,
        gate_pre,
        grad_out_in,
        hidden_low,
        entered,
        readers,
        start,
        output_full,
        gain_full,
        skip_wide,
    )
    block_output = lax.all_gather(block_rows, "head").reshape(rows, block, width)
    grad_output_weight = reduce_weight(from_rows(dot_rows(out_in, cot), head_devices))
    grad_gate_weight = reduce_weight(from_columns(dot_rows(normed, grad_gate), head_devices))
    grad_end = carried(passing_wide, grad_start, rows, chunk, True)
    grad_mixed, sums, grad_states, state_sums, rate, direct = run_back(
        x,
        mixed,
        run,
        size,
        grad_scan,
        total,
        grad_end,
        start,
        kernel_rows,
        bias_full,
        skip_wide,
        states,
        kernel_state,
        bias_state_row,
        masks,
        seg_col,
        seg_row,
        writers,
        readers,
        turned,
        grad_read,
    )
    edge_values = chunk_permute(grad_mixed[HALO - 8 : HALO], rows, lambda c: c - 1)
    edge_states = chunk_permute(grad_states[HALO - 8 : HALO], rows, lambda c: c - 1)
    fill = ((length - 8, 0), (0, 0))
    grad_values_in = (grad_mixed[HALO:] + jnp.pad(edge_values, fill)).astype(BF16)
    grad_states_in = (grad_states[HALO:] + jnp.pad(edge_states, fill)).astype(BF16)

    kept = jnp.stack([sums[6].reshape(-1, LANES).sum(1), sums[7].reshape(-1, LANES).sum(1)], axis=1)
    rate_end = sums[5].reshape(heads, HEADDIM).sum(1) + passing * kept.reshape(heads)
    grad_log_decay = rate[:, :heads] + rate_end
    grad_step_size = direct[:, :heads] - grad_log_decay * decay_full
    grad_step_raw = grad_step_size * jax.nn.sigmoid(step_raw)
    grad_step_in = grad_step_raw.astype(BF16)
    grad_decay_log = jnp.sum(grad_log_decay * log_decay, axis=0)
    grad_step_bias = jnp.sum(grad_step_raw, axis=0)
    grad_skip_gain = gate_sums[1].reshape(heads, HEADDIM).sum(1)

    grad_normed = (
        dot_turned(grad_gate, gate_full)
        + dot_turned(grad_values_in, value_full)
        + dot_turned(grad_states_in, state_weight)
        + dot_turned(grad_step_in, step_full)
    )
    grad_norm_gain = jnp.sum(grad_normed * hidden * norm_scale, axis=0)
    grad_unit = grad_normed * norm_gain
    change = norm_scale * grad_unit - hidden * norm_scale**3 * jnp.mean(
        grad_unit * hidden, axis=1, keepdims=True
    )
    changes = lax.all_gather(change.astype(BF16), "head").reshape(rows, block, width)
    input_gradient = cotangent.astype(F32) + changes.astype(F32)

    grad_value_weight = reduce_weight(
        from_columns(dot_rows(normed, grad_values_in), head_devices)
    )
    grad_state_weight = dot_rows(normed, grad_states_in)
    grad_step_weight = dot_rows(normed, grad_step_in)
    pieces = [
        grad_state_weight,
        grad_step_weight,
        grad_norm_gain,
        sums[:taps],
        state_sums[:taps],
        sums[4],
        state_sums[4],
        grad_step_bias,
        grad_decay_log,
        grad_skip_gain,
        gate_sums[0],
    ]
    flat = jnp.concatenate([piece.reshape(-1) for piece in pieces]).astype(BF16)
    unit = lax.axis_size("seq") * 16 * LANES
    padded = -(-flat.shape[0] // unit) * unit
    flat = jnp.pad(flat, (0, padded - flat.shape[0])).reshape(-1, LANES)
    flat = reduce_all(flat).reshape(-1).astype(F32)
    summed, at = [], 0
    for piece in pieces:
        summed.append(flat[at : at + piece.size].reshape(piece.shape))
        at += piece.size

    def own(value, axis):
        size = value.shape[axis] // head_devices
        return lax.dynamic_slice_in_dim(value, head_index * size, size, axis)

    return (
        block_output,
        input_gradient,
        summed[2],
        grad_gate_weight.astype(F32),
        grad_value_weight.astype(F32),
        summed[0],
        own(summed[1], 1),
        own(summed[3], 1),
        summed[4],
        own(summed[5], 0),
        summed[6],
        own(summed[7], 0),
        own(summed[8], 0),
        own(summed[9], 0),
        own(summed[10], 0),
        grad_output_weight.astype(F32),
    )


def solution(mesh):
    placed = (
        P(None, "seq", None),
        P(),
        P(),
        P(None, "head"),
        P(None, "head"),
        P(),
        P(None, "head"),
        P(None, "head"),
        P(),
        P("head"),
        P(),
        P("head"),
        P("head"),
        P("head"),
        P("head"),
        P("head", None),
        P(None, "seq", None),
    )
    return jax.shard_map(
        shards,
        mesh=mesh,
        in_specs=placed,
        out_specs=(
            P(None, "seq", None),
            P(None, "seq", None),
            P(),
            P(None, "head"),
            P(None, "head"),
            P(),
            P(None, "head"),
            P(None, "head"),
            P(),
            P("head"),
            P(),
            P("head"),
            P("head"),
            P("head"),
            P("head"),
            P("head", None),
        ),
        check_vma=False,
    )
```

```python
import functools

import jax
import jax.numpy as jnp
from jax import lax
from jax.experimental import pallas as pl
from jax.experimental.pallas import tpu as pltpu
from jax.sharding import PartitionSpec as P

HEADDIM = 64
STATE = 128
EPSILON = 1e-05
HIGHEST = lax.Precision.HIGHEST
LANES = 128
HALO = 16
TILE = 256
BF16 = jnp.bfloat16
F32 = jnp.float32
VMEM_LIMIT = 56 * 1024 * 1024


def bits_of(count):
    return count.bit_length() - 1


def swap(value, axis, bit):
    count = lax.axis_size(axis)
    return lax.ppermute(value, axis, [(i, i ^ (1 << bit)) for i in range(count)])


def bit_of(axis, bit):
    return (lax.axis_index(axis) >> bit) & 1


def joined(mine, other, upper, axis):
    return jnp.where(
        upper == 1,
        jnp.concatenate([other, mine], axis=axis),
        jnp.concatenate([mine, other], axis=axis),
    )


def swap_orders():
    bits = bits_of(lax.axis_size("seq"))
    return list(range(1, bits)), list(reversed(range(1, bits)))


def seq_rank(order):
    return sum(bit_of("seq", b) << (len(order) - 1 - i) for i, b in enumerate(order))


def join_seq(value, bit, axis):
    return joined(value, swap(value, "seq", bit), bit_of("seq", bit), axis)


def gather_blocks(value):
    count, place = lax.axis_size("head"), lax.axis_index("head")
    blocks = [value]
    for d in range(1, count):
        pairs = [(i, (i + d) % count) for i in range(count)]
        blocks.insert(0, lax.ppermute(value, "head", pairs))
    blocks = lax.dynamic_slice_in_dim(jnp.stack(blocks + blocks), count - 1 - place, count, 0)
    return [blocks[h] for h in range(count)]


def three_parts(value):
    parts = []
    for _ in range(3):
        part = lax.reduce_precision(value, 8, 7)
        parts.append(part.astype(BF16))
        value = value - part
    return parts


def gather_columns(weight, extra):
    first, second = swap_orders()
    half, columns = weight.shape[0] // 2, weight.shape[1]
    part = half // lax.axis_size("seq")
    lines = -(-extra.shape[0] // (16 * columns)) * 16
    extra_rows = jnp.pad(extra, (0, lines * columns - extra.shape[0])).reshape(lines, columns)
    own = [
        lax.dynamic_slice_in_dim(weight, at + seq_rank([0] + order) * part, part, 0)
        for at, order in ((0, first), (half, second))
    ]
    blocks = gather_blocks(jnp.concatenate([*own, extra_rows], axis=0))
    whole = jnp.concatenate([block[: 2 * part] for block in blocks], axis=1)
    extras = jnp.stack([block[2 * part :].reshape(-1)[: extra.shape[0]] for block in blocks])
    upper, lower = whole[:part], whole[part:]
    for a, b in zip(reversed(first), reversed(second)):
        upper, lower = join_seq(upper, a, 0), join_seq(lower, b, 0)
    whole = join_seq(jnp.stack([upper, lower]), 0, 1)
    return whole.reshape(weight.shape[0], whole.shape[2]), extras


def halve(value, name, bit, axis):
    size = value.shape[axis] // 2
    upper = bit_of(name, bit)
    keep = lax.dynamic_slice_in_dim(value, upper * size, size, axis)
    send = lax.dynamic_slice_in_dim(value, (1 - upper) * size, size, axis)
    got = swap(send, name, bit)
    return (keep.astype(F32) + got.astype(F32)).astype(value.dtype)


def split_blocks(value, size):
    count = value.shape[-1] // size
    return jnp.stack([value[..., h * size : (h + 1) * size] for h in range(count)])


def sum_blocks_step(blocks, shared, bit):
    count = blocks.shape[0]
    pairs = blocks.reshape((count // 2, 2) + blocks.shape[1:])
    upper = bit_of("head", bit)
    keep = lax.dynamic_index_in_dim(pairs, upper, 1, keepdims=False)
    send = lax.dynamic_index_in_dim(pairs, 1 - upper, 1, keepdims=False)
    shape = keep.shape
    keep = jnp.concatenate([keep.reshape((-1,) + shape[2:]), shared], axis=0)
    send = jnp.concatenate([send.reshape((-1,) + shape[2:]), shared], axis=0)
    total = (keep.astype(F32) + swap(send, "head", bit).astype(F32)).astype(blocks.dtype)
    most = shape[0] * shape[1]
    return total[:most].reshape(shape), total[most:]


def chunk_permute(value, rows, target):
    seq_count, head_count = lax.axis_size("seq"), lax.axis_size("head")
    parts = head_count // rows
    pairs = []
    for s in range(seq_count):
        for h in range(head_count):
            goal = target(s * parts + h % parts)
            if 0 <= goal < seq_count * parts:
                place = (goal // parts) * head_count + (h // parts) * parts + goal % parts
                pairs.append((s * head_count + h, place))
    return lax.ppermute(value, ("seq", "head"), pairs)


def carried(rate, state, rows, chunk, reverse, meanwhile):
    count = lax.axis_size("seq") * (lax.axis_size("head") // rows)
    levels = bits_of(count)
    size = state.shape[0] // 2
    heads = rate.shape[0]
    side = chunk & 1
    done = []

    def exchange(value, rate, level, step):
        coarse = lax.reduce_precision(rate, 8, 7)
        fine = (rate - coarse).astype(BF16)
        coarse = coarse.astype(BF16)
        tail = jnp.pad(jnp.stack([coarse, fine]), ((0, 14), (0, STATE - heads)))
        message = jnp.concatenate([value.astype(BF16), tail], axis=0)
        got = chunk_permute(message, rows, lambda c: c ^ (1 << level))
        got, extra = lax.optimization_barrier((got, meanwhile[step]() if step < len(meanwhile) else ()))
        done.append(extra)
        pair = got[size : size + 2, :heads].astype(F32)
        return got[:size].astype(F32), pair[0] + pair[1]

    def widen(rate):
        return lax.dynamic_slice_in_dim(jnp.repeat(rate, HEADDIM), side * size, size, 0)[:, None]

    low = state.astype(BF16)
    send = lax.dynamic_slice_in_dim(low, (1 - side) * size, size, 0)
    mine = lax.dynamic_slice_in_dim(state, side * size, size, 0)
    theirs, their_rate = exchange(send, rate, 0, 0)
    comes_second = side == (0 if reverse else 1)
    earlier = jnp.where(comes_second, theirs, mine)
    later = jnp.where(comes_second, mine, theirs)
    first_rate = jnp.where(comes_second, their_rate, rate)
    second_rate = jnp.where(comes_second, rate, their_rate)
    total = widen(second_rate) * earlier + later
    total_rate = rate * their_rate
    before = jnp.zeros_like(total)
    before_rate = jnp.ones_like(rate)
    for b in range(1, levels):
        got, got_rate = exchange(total, total_rate, b, b)
        after = ((chunk >> b) & 1) == (0 if reverse else 1)
        before = jnp.where(after, widen(before_rate) * got + before, before)
        before_rate = jnp.where(after, before_rate * got_rate, before_rate)
        if b < levels - 1:
            total = jnp.where(
                after, widen(total_rate) * got + total, widen(got_rate) * total + got
            )
            total_rate = total_rate * got_rate
    second = widen(first_rate) * before + earlier
    own = jnp.where(comes_second, second, before).astype(BF16)
    other = jnp.where(comes_second, before, second).astype(BF16)
    got = chunk_permute(other, rows, lambda c: c ^ 1)
    return joined(own, got, side, 0), done


def contract(a, b, dims):
    return lax.dot_general(a, b, ((dims[0], dims[1]), ((), ())), preferred_element_type=F32)


def taps_of(padded, masks):
    taps = []
    for k in range(4):
        moved = padded if k == 3 else pltpu.roll(padded, 3 - k, 0)
        tap = moved[HALO:]
        taps.append(tap if k == 3 else tap * masks[:, k : k + 1])
    return taps


def summed_of(taps, kernel, bias):
    summed = bias
    for k in range(4):
        summed = summed + kernel[k : k + 1, :] * taps[k]
    return summed


def linked_of(seg_col, seg_row):
    length = seg_col.shape[0]
    row = lax.broadcasted_iota(jnp.int32, (length, length), 0)
    col = lax.broadcasted_iota(jnp.int32, (length, length), 1)
    return jnp.where((row >= col) & (seg_col == seg_row), 1.0, 0.0)


def blocks_of(length):
    count = length // TILE
    return [(t, s) for t in range(count) for s in range(t + 1)]


def cut(index):
    return slice(index * TILE, (index + 1) * TILE)


def scan_kernel(
    mixed_ref,
    states_ref,
    kernel_ref,
    bias_ref,
    kernel_state_ref,
    bias_state_ref,
    masks_ref,
    seg_col_ref,
    seg_row_ref,
    step_ref,
    decay_ref,
    x_ref,
    open_ref,
    end_ref,
    run_ref,
    size_ref,
    writers_ref,
    readers_ref,
    turned_ref,
    scores,
    run_all,
    size_all,
):
    pair = pl.program_id(0)
    length = x_ref.shape[0]
    pairs = run_all.shape[0]
    low = lax.broadcasted_iota(jnp.int32, (1, LANES), 1) < HEADDIM
    masks = masks_ref[...]

    @pl.when(pair == 0)
    def _():
        taps = taps_of(states_ref[...].astype(F32), masks)
        summed = summed_of(taps, kernel_state_ref[...], bias_state_ref[...])
        active = (summed * jax.nn.sigmoid(summed)).astype(BF16)
        writers = active[:, :STATE]
        readers = active[:, STATE:]
        writers_ref[...] = writers
        readers_ref[...] = readers
        linked = linked_of(seg_col_ref[...], seg_row_ref[...])
        scores[...] = contract(readers, writers, ((1,), (1,))) * linked
        row = lax.broadcasted_iota(jnp.int32, (length, length), 0)
        col = lax.broadcasted_iota(jnp.int32, (length, length), 1)
        lower = jnp.where(row >= col, 1.0, 0.0)
        run = jnp.dot(lower, decay_ref[...], precision=HIGHEST, preferred_element_type=F32)
        turned_ref[...] = run.T
        size = step_ref[...]
        for i in range(pairs):
            a, b = 2 * i, 2 * i + 1
            run_all[i] = jnp.where(low, run[:, a : a + 1], run[:, b : b + 1])
            size_all[i] = jnp.where(low, size[:, a : a + 1], size[:, b : b + 1])

    run = run_all[pair]
    size = size_all[pair]
    run_ref[...] = run
    size_ref[...] = size
    taps = taps_of(mixed_ref[...].astype(F32), masks)
    summed = summed_of(taps, kernel_ref[...], bias_ref[...])
    x = (summed * jax.nn.sigmoid(summed)).astype(BF16)
    x_ref[...] = x
    sized = x.astype(F32) * size
    sized_low = sized.astype(BF16)
    zero = jnp.zeros((), BF16)
    halves = (jnp.where(low, sized_low, zero), jnp.where(low, zero, sized_low))
    totals = [None] * (length // TILE)
    for t, s in blocks_of(length):
        score = scores[cut(t), cut(s)]
        for j in range(2):
            row = turned_ref[pl.ds(2 * pair + j, 1), :][:, cut(s)]
            col = run[cut(t), j * HEADDIM : j * HEADDIM + 1]
            weight = (score * jnp.exp(jnp.minimum(col - row, 0.0))).astype(BF16)
            part = contract(weight, halves[j][cut(s)], ((1,), (0,)))
            totals[t] = part if totals[t] is None else totals[t] + part
    for t, total in enumerate(totals):
        open_ref[cut(t), :] = total
    seg_col = seg_col_ref[...]
    last = jnp.where(seg_col == seg_col[length - 1 : length, :], 1.0, 0.0)
    toward = last * jnp.exp(run[length - 1 : length, :] - run)
    end_ref[...] = contract((toward * sized).astype(BF16), writers_ref[...], ((0,), (0,)))


def gate_kernel(
    open_ref,
    x_ref,
    run_ref,
    gate_ref,
    grad_out_ref,
    hidden_ref,
    entered_ref,
    readers_ref,
    start_ref,
    weight_ref,
    gain_ref,
    skip_ref,
    total_ref,
    out_in_ref,
    block_ref,
    grad_scan_ref,
    grad_gate_ref,
    grad_read_ref,
    sums_ref,
    grad_start_ref,
):
    step = pl.program_id(0)
    inner = gain_ref.shape[1]
    gain = gain_ref[...]
    x = x_ref[...].astype(F32)
    start = start_ref[...]
    readers = readers_ref[...]
    reach = entered_ref[...] * jnp.exp(run_ref[...])
    total = open_ref[...] + reach * contract(readers, start, ((1,), (1,)))
    total_ref[...] = total
    scanned = total + skip_ref[...] * x
    gate = gate_ref[...]
    sig = jax.nn.sigmoid(gate)
    act = gate * sig
    gated = scanned * act
    scale = lax.rsqrt(jnp.sum(gated * gated, axis=1, keepdims=True) / inner + EPSILON)
    unit = gated * scale
    out_in = (unit * gain).astype(BF16)
    out_in_ref[...] = out_in
    branch = contract(out_in, weight_ref[...], ((1,), (0,)))
    block_ref[...] = (hidden_ref[...].astype(F32) + branch).astype(BF16)
    grad_out = grad_out_ref[...]
    q = grad_out * gain
    inner_product = jnp.sum(q * gated, axis=1, keepdims=True) / inner
    grad_gated = scale * q - gated * (scale * scale * scale * inner_product)
    grad_scan = grad_gated * act
    grad_scan_low = grad_scan.astype(BF16)
    grad_scan_ref[...] = grad_scan_low
    slope = sig * (1.0 + gate * (1.0 - sig))
    grad_gate_ref[...] = (grad_gated * scanned * slope).astype(BF16)
    reached = (reach * grad_scan).astype(BF16)
    grad_read_ref[...] = contract(reached, start, ((1,), (0,)))
    grad_start = contract(reached, readers, ((0,), (0,)))
    gain_sum = jnp.sum(grad_out * unit, axis=0, keepdims=True)
    skip_sum = jnp.sum(grad_scan * x, axis=0, keepdims=True)
    rows = lax.broadcasted_iota(jnp.int32, (8, inner), 0)
    sums = jnp.where(rows == 0, gain_sum, jnp.where(rows == 1, skip_sum, 0.0))

    @pl.when(step == 0)
    def _():
        sums_ref[...] = sums
        grad_start_ref[...] = grad_start

    @pl.when(step > 0)
    def _():
        sums_ref[...] += sums
        grad_start_ref[...] += grad_start


def first_pair(first, count):
    return 0 if first else count


def conv_back(grad_act, padded, kernel, bias, masks):
    length, width = grad_act.shape
    taps = taps_of(padded, masks)
    summed = summed_of(taps, kernel, bias)
    sig = jax.nn.sigmoid(summed)
    grad_u = grad_act * (sig * (1.0 + summed * (1.0 - sig)))
    rows = lax.broadcasted_iota(jnp.int32, (8, width), 0)
    sums = jnp.where(rows == 4, jnp.sum(grad_u, axis=0, keepdims=True), 0.0)
    mixed = None
    nothing = jnp.zeros((HALO, width), F32)
    for k in range(4):
        sums = jnp.where(rows == k, jnp.sum(grad_u * taps[k], axis=0, keepdims=True), sums)
        back = grad_u * kernel[k : k + 1, :]
        if k < 3:
            back = back * masks[:, k : k + 1]
        back = jnp.concatenate([nothing, back], axis=0)
        if k < 3:
            back = pltpu.roll(back, length + HALO - (3 - k), 0)
        mixed = back if mixed is None else mixed + back
    return mixed, sums


def back_kernel(first, last, *refs):
    (
        x_ref,
        mixed_ref,
        run_ref,
        size_ref,
        grad_scan_ref,
        total_ref,
        grad_end_ref,
        start_ref,
        kernel_ref,
        bias_ref,
        skip_ref,
        masks_ref,
        seg_col_ref,
        seg_row_ref,
        writers_ref,
        readers_ref,
        turned_ref,
    ) = refs[:17]
    refs = refs[17:]
    if last:
        states_ref, kernel_state_ref, bias_state_ref, grad_read_ref = refs[:4]
        refs = refs[4:]
    sums_in = () if first else refs[:4]
    refs = refs[len(sums_in) :]
    grad_mixed_ref, sums_ref = refs[:2]
    refs = refs[2:]
    scores, grad_scores, grad_write, rate_sum, direct_sum = refs[-5:]
    refs = refs[:-5]
    if last:
        grad_states_ref, sums_state_ref, rate_ref, direct_ref = refs
    place = pl.program_id(0)
    pair = place + first_pair(first, pl.num_programs(0))
    length = x_ref.shape[0]
    low = lax.broadcasted_iota(jnp.int32, (1, LANES), 1) < HEADDIM
    lane = lax.broadcasted_iota(jnp.int32, (1, LANES), 1)
    masks = masks_ref[...]
    writers = writers_ref[...]
    readers = readers_ref[...]
    seg_col = seg_col_ref[...]

    totals = (grad_scores, grad_write, rate_sum, direct_sum)

    @pl.when(place == 0)
    def _():
        linked = linked_of(seg_col, seg_row_ref[...])
        scores[...] = contract(readers, writers, ((1,), (1,))) * linked
        for i, total in enumerate(totals):
            total[...] = jnp.zeros_like(total) if first else sums_in[i][...]

    run = run_ref[...]
    size = size_ref[...]
    x = x_ref[...].astype(F32)
    sized = x * size
    sized_low = sized.astype(BF16)
    grad_scan = grad_scan_ref[...]
    zero = jnp.zeros((), BF16)
    halves = (jnp.where(low, grad_scan, zero), jnp.where(low, zero, grad_scan))
    inner = [None] * (length // TILE)
    for t, s in blocks_of(length):
        score = scores[cut(t), cut(s)]
        grad_score = grad_scores[cut(t), cut(s)]
        for j in range(2):
            row = turned_ref[pl.ds(2 * pair + j, 1), :][:, cut(s)]
            col = run[cut(t), j * HEADDIM : j * HEADDIM + 1]
            decay = jnp.exp(jnp.minimum(col - row, 0.0))
            weight = (score * decay).astype(BF16)
            grad_weight = contract(halves[j][cut(t)], sized_low[cut(s)], ((1,), (1,)))
            grad_score = grad_score + grad_weight * decay
            part = contract(weight, halves[j][cut(t)], ((0,), (0,)))
            inner[s] = part if inner[s] is None else inner[s] + part
        grad_scores[cut(t), cut(s)] = grad_score
    inner = inner[0] if len(inner) == 1 else jnp.concatenate(inner, axis=0)
    final = jnp.where(seg_col == seg_col[length - 1 : length, :], 1.0, 0.0)
    toward = final * jnp.exp(run[length - 1 : length, :] - run)
    grad_end = grad_end_ref[...]
    outer = toward * contract(writers, grad_end.astype(BF16), ((1,), (1,)))
    grad_write[...] += contract(
        (toward * sized).astype(BF16), grad_end.astype(BF16), ((1,), (0,))
    )
    grad_sized = inner + outer
    grad_scan = grad_scan.astype(F32)
    sized_low = sized_low.astype(F32)
    change = grad_scan * total_ref[...] - sized_low * grad_sized
    straight = x * grad_sized
    for j in range(2):
        side = low if j == 0 else jnp.logical_not(low)
        here = lane == 2 * pair + j
        one = jnp.sum(jnp.where(side, change, 0.0), axis=1, keepdims=True)
        rate_sum[...] += jnp.where(here, one, 0.0)
        two = jnp.sum(jnp.where(side, straight, 0.0), axis=1, keepdims=True)
        direct_sum[...] += jnp.where(here, two, 0.0)
    grad_x = size * grad_sized + skip_ref[...] * grad_scan
    grad_mixed, sums = conv_back(
        grad_x, mixed_ref[...].astype(F32), kernel_ref[...], bias_ref[...], masks
    )
    grad_mixed_ref[...] = grad_mixed
    rows = lax.broadcasted_iota(jnp.int32, (8, LANES), 0)
    outer_sum = jnp.sum(sized_low * outer, axis=0, keepdims=True)
    kept = start_ref[...].astype(F32) * grad_end
    kept_low = jnp.sum(kept[:HEADDIM], axis=0, keepdims=True)
    kept_high = jnp.sum(kept[HEADDIM:], axis=0, keepdims=True)
    sums = jnp.where(rows == 5, outer_sum, sums)
    sums = jnp.where(rows == 6, kept_low, jnp.where(rows == 7, kept_high, sums))
    sums_ref[...] = sums

    @pl.when(place == pl.num_programs(0) - 1)
    def _():
        if not last:
            for ref, total in zip(refs, totals):
                ref[...] = total[...]
            return
        linked = linked_of(seg_col, seg_row_ref[...])
        grad_score = (grad_scores[...] * linked).astype(BF16)
        grad_readers = contract(grad_score, writers, ((1,), (0,))) + grad_read_ref[...]
        grad_writers = contract(grad_score, readers, ((0,), (0,))) + grad_write[...]
        grad_act = jnp.concatenate([grad_writers, grad_readers], axis=1)
        grad_states, state_sums = conv_back(
            grad_act,
            states_ref[...].astype(F32),
            kernel_state_ref[...],
            bias_state_ref[...],
            masks,
        )
        grad_states_ref[...] = grad_states
        sums_state_ref[...] = state_sums
        row = lax.broadcasted_iota(jnp.int32, (length, length), 0)
        col = lax.broadcasted_iota(jnp.int32, (length, length), 1)
        upper = jnp.where(col >= row, 1.0, 0.0)
        rate_ref[...] = jnp.dot(
            upper, rate_sum[...], precision=HIGHEST, preferred_element_type=F32
        )
        direct_ref[...] = direct_sum[...]


def whole_spec(shape):
    return pl.BlockSpec(shape, lambda i: (0,) * len(shape))


def columns_spec(rows):
    return pl.BlockSpec((rows, LANES), lambda i: (0, i))


def rows_spec(rows, width):
    return pl.BlockSpec((rows, width), lambda i: (i, 0))


def run_scan(mixed, states, kernel, bias, kernel_state, bias_state, masks, seg_col, seg_row, step, decay):
    length = mixed.shape[0] - HALO
    inner = mixed.shape[1]
    pairs = inner // LANES
    wide = 2 * STATE
    return pl.pallas_call(
        scan_kernel,
        grid=(pairs,),
        in_specs=[
            columns_spec(length + HALO),
            whole_spec((length + HALO, wide)),
            columns_spec(4),
            columns_spec(1),
            whole_spec((4, wide)),
            whole_spec((1, wide)),
            whole_spec((length, 4)),
            whole_spec((length, 1)),
            whole_spec((1, length)),
            whole_spec((length, LANES)),
            whole_spec((length, LANES)),
        ],
        out_specs=[
            columns_spec(length),
            columns_spec(length),
            rows_spec(LANES, STATE),
            columns_spec(length),
            columns_spec(length),
            whole_spec((length, STATE)),
            whole_spec((length, STATE)),
            whole_spec((LANES, length)),
        ],
        out_shape=[
            jax.ShapeDtypeStruct((length, inner), BF16),
            jax.ShapeDtypeStruct((length, inner), F32),
            jax.ShapeDtypeStruct((inner, STATE), F32),
            jax.ShapeDtypeStruct((length, inner), F32),
            jax.ShapeDtypeStruct((length, inner), F32),
            jax.ShapeDtypeStruct((length, STATE), BF16),
            jax.ShapeDtypeStruct((length, STATE), BF16),
            jax.ShapeDtypeStruct((LANES, length), F32),
        ],
        scratch_shapes=[
            pltpu.VMEM((length, length), F32),
            pltpu.VMEM((pairs, length, LANES), F32),
            pltpu.VMEM((pairs, length, LANES), F32),
        ],
        compiler_params=pltpu.CompilerParams(vmem_limit_bytes=VMEM_LIMIT),
        name="scan_forward",
    )(mixed, states, kernel, bias, kernel_state, bias_state, masks, seg_col, seg_row, step, decay)


def run_gate(opened, x, run, gate, grad_out, hidden, entered, readers, start, weight, gain, skip):
    length, inner = x.shape
    width = hidden.shape[1]
    tile = 128
    return pl.pallas_call(
        gate_kernel,
        grid=(length // tile,),
        in_specs=[
            rows_spec(tile, inner),
            rows_spec(tile, inner),
            rows_spec(tile, inner),
            rows_spec(tile, inner),
            rows_spec(tile, inner),
            rows_spec(tile, width),
            rows_spec(tile, 1),
            rows_spec(tile, STATE),
            whole_spec((inner, STATE)),
            whole_spec((inner, width)),
            whole_spec((1, inner)),
            whole_spec((1, inner)),
        ],
        out_specs=[
            rows_spec(tile, inner),
            rows_spec(tile, inner),
            rows_spec(tile, width),
            rows_spec(tile, inner),
            rows_spec(tile, inner),
            rows_spec(tile, STATE),
            whole_spec((8, inner)),
            whole_spec((inner, STATE)),
        ],
        out_shape=[
            jax.ShapeDtypeStruct((length, inner), F32),
            jax.ShapeDtypeStruct((length, inner), BF16),
            jax.ShapeDtypeStruct((length, width), BF16),
            jax.ShapeDtypeStruct((length, inner), BF16),
            jax.ShapeDtypeStruct((length, inner), BF16),
            jax.ShapeDtypeStruct((length, STATE), F32),
            jax.ShapeDtypeStruct((8, inner), F32),
            jax.ShapeDtypeStruct((inner, STATE), F32),
        ],
        compiler_params=pltpu.CompilerParams(vmem_limit_bytes=VMEM_LIMIT),
        name="gate_both",
    )(opened, x, run, gate, grad_out, hidden, entered, readers, start, weight, gain, skip)


def run_back(first, wide_args, rows_args, row_args, whole_args, last_args, sums_in):
    x = wide_args[0]
    length, inner = x.shape
    wide = 2 * STATE
    pairs = inner // LANES
    at = 0
    last = True

    def columns(rows, offset):
        return pl.BlockSpec((rows, LANES), lambda i: (0, i + offset))

    args = [*wide_args, *rows_args, *row_args, *whole_args, *last_args, *sums_in]
    in_specs = (
        [columns(a.shape[0], at) for a in wide_args]
        + [pl.BlockSpec((LANES, STATE), lambda i: (i + at, 0)) for a in rows_args]
        + [columns(a.shape[0], at) for a in row_args]
        + [whole_spec(a.shape) for a in (*whole_args, *last_args, *sums_in)]
    )
    sum_shapes = [(length, length), (length, STATE), (length, LANES), (length, LANES)]
    out_shapes = [(length + HALO, inner), (8, inner)]
    out_specs = [columns(length + HALO, 0), columns(8, 0)]
    more = [(length + HALO, wide), (8, wide), (length, LANES), (length, LANES)] if last else sum_shapes
    out_specs += [whole_spec(shape) for shape in more]
    return pl.pallas_call(
        functools.partial(back_kernel, first, last),
        grid=(pairs,),
        in_specs=in_specs,
        out_specs=out_specs,
        out_shape=[jax.ShapeDtypeStruct(shape, F32) for shape in out_shapes + more],
        scratch_shapes=[pltpu.VMEM((length, length), F32)]
        + [pltpu.VMEM(shape, F32) for shape in sum_shapes],
        compiler_params=pltpu.CompilerParams(vmem_limit_bytes=VMEM_LIMIT),
        name="scan_backward",
    )(*args)


def dot(a, b):
    return jnp.dot(a, b, preferred_element_type=F32)


def dot_rows(a, b):
    return lax.dot_general(a, b, (((0,), (0,)), ((), ())), preferred_element_type=F32)


def dot_turned(a, b):
    return lax.dot_general(a, b, (((1,), (1,)), ((), ())), preferred_element_type=F32)


def pad_lanes(value):
    return jnp.pad(value, ((0, 0), (0, LANES - value.shape[1])))


def shards(
    hidden_states,
    segment_ids,
    norm_gain,
    gate_weight,
    value_weight,
    state_weight,
    step_weight,
    kernel_value,
    kernel_state,
    bias_value,
    bias_state,
    step_bias,
    decay_log,
    skip_gain,
    inner_gain,
    output_weight,
    cotangent,
):
    rows, block, width = hidden_states.shape
    head_devices = lax.axis_size("head")
    parts = head_devices // rows
    length = block // parts
    seq_index, head_index = lax.axis_index("seq"), lax.axis_index("head")
    row_index, part_index = head_index // parts, head_index % parts
    chunk = seq_index * parts + part_index
    local_inner = gate_weight.shape[1]
    local_heads = step_bias.shape[0]
    inner = local_inner * head_devices
    heads = local_heads * head_devices
    taps = kernel_value.shape[0]

    small = jnp.concatenate(
        [kernel_value.reshape(-1), bias_value, inner_gain, step_bias, decay_log, skip_gain]
    )
    count = small.shape[0]
    value_full, extras = gather_columns(
        value_weight, jnp.concatenate([*three_parts(small), step_weight.reshape(-1)])
    )
    small = sum(extras[:, i * count : (i + 1) * count].astype(F32) for i in range(3))
    step_full = extras[:, 3 * count :].reshape(head_devices, width, local_heads)
    step_full = step_full.transpose(1, 0, 2).reshape(width, heads)
    seq_count = lax.axis_size("seq")
    part = width // seq_count
    out_part = local_inner // seq_count
    packed = jnp.concatenate(
        [
            lax.dynamic_slice_in_dim(gate_weight, seq_index * part, part, 0),
            lax.dynamic_slice_in_dim(output_weight, seq_index * out_part, out_part, 0).reshape(
                part, local_inner
            ),
        ],
        axis=0,
    )
    packed = lax.all_gather(packed, ("seq", "head"))
    packed = packed.reshape(seq_count, head_devices, 2 * part, local_inner)
    at = taps * local_inner
    kernel_full = small[:, :at].reshape(head_devices, taps, local_inner)
    kernel_full = kernel_full.transpose(1, 0, 2).reshape(taps, inner)
    bias_full = small[:, at : at + local_inner].reshape(1, inner)
    at += local_inner
    gain_full = small[:, at : at + local_inner].reshape(1, inner)
    at += local_inner
    step_bias_full = small[:, at : at + local_heads].reshape(heads)
    at += local_heads
    decay_full = jnp.exp(small[:, at : at + local_heads].reshape(heads))
    at += local_heads
    skip_full = small[:, at : at + local_heads].reshape(heads)
    skip_wide = jnp.repeat(skip_full, HEADDIM)[None]

    place = (row_index, part_index * length, 0)
    hidden_low = lax.dynamic_slice(hidden_states, place, (1, length, width))[0]
    cot = lax.dynamic_slice(cotangent, place, (1, length, width))[0]
    edge = chunk_permute(hidden_low[length - HALO :], rows, lambda c: c + 1)
    hidden_ext = jnp.concatenate([edge, hidden_low], axis=0).astype(F32)
    scale_ext = lax.rsqrt(jnp.mean(hidden_ext * hidden_ext, axis=1, keepdims=True) + EPSILON)
    normed_ext = (hidden_ext * scale_ext * norm_gain).astype(BF16)
    normed = normed_ext[HALO:]
    hidden = hidden_low.astype(F32)
    norm_scale = scale_ext[HALO:]

    seg_line = lax.dynamic_slice_in_dim(segment_ids, row_index, 1, 0)[0]
    seg_line = jnp.concatenate([jnp.full((HALO,), -1, jnp.int32), seg_line])
    window = lax.dynamic_slice_in_dim(seg_line, chunk * length, length + HALO, 0)
    segments = window[HALO:]
    before = window[HALO - 1]
    masks = jnp.stack(
        [window[HALO - 3 + k : HALO - 3 + k + length] == segments for k in range(taps)], axis=1
    ).astype(F32)
    entered = (segments == before).astype(F32)[:, None]
    seg_col = segments.astype(F32)[:, None]
    seg_row = segments.astype(F32)[None]

    mixed = dot(normed_ext, value_full).astype(BF16)
    states = dot(normed_ext, state_weight).astype(BF16)
    step_raw = dot(normed, step_full) + step_bias_full
    step_size = jax.nn.softplus(step_raw)
    log_decay = -step_size * decay_full
    passing = jnp.exp(jnp.sum(log_decay, axis=0)) * (segments[length - 1] == before).astype(F32)

    kernel_rows = kernel_full
    bias_state_row = bias_state[None]
    x, opened, end_state, run, size, writers, readers, turned = run_scan(
        mixed,
        states,
        kernel_rows,
        bias_full,
        kernel_state,
        bias_state_row,
        masks,
        seg_col,
        seg_row,
        pad_lanes(step_size),
        pad_lanes(log_decay),
    )
    def make_gate():
        gate_full = packed[:, :, :part].transpose(0, 2, 1, 3).reshape(width, inner)
        return gate_full, dot(normed, gate_full)

    def make_out():
        output_full = packed[:, :, part:].reshape(seq_count, head_devices, out_part, width)
        output_full = output_full.transpose(1, 0, 2, 3).reshape(inner, width)
        return output_full, dot_turned(cot, output_full)

    start, done = carried(
        passing, end_state, rows, chunk, False, (tuple, make_gate, make_out)
    )
    gate_full, gate_pre = done[1]
    output_full, grad_out_in = done[2]
    total, out_in, block_rows, grad_scan, grad_gate, grad_read, gate_sums, grad_start = run_gate(
        opened,
        x,
        run,
        gate_pre,
        grad_out_in,
        hidden_low,
        entered,
        readers,
        start,
        output_full,
        gain_full,
        skip_wide,
    )
    block_output = lax.all_gather(block_rows, "head").reshape(rows, block, width)
    first, second = swap_orders()

    def early_start():
        return (
            halve(dot_rows(cot, out_in).astype(BF16), "seq", 0, 0),
            halve(dot_rows(normed, grad_gate).astype(BF16), "seq", 0, 0),
            dot_turned(grad_gate, gate_full),
        )

    grad_end, done = carried(passing, grad_start, rows, chunk, True, (tuple, early_start))
    out_grad, gate_grad, grad_normed = done[1]
    out_grad, gate_grad, grad_end = lax.optimization_barrier((out_grad, gate_grad, grad_end))
    out_grad = halve(out_grad, "seq", first[0], 0)
    gate_grad = halve(gate_grad, "seq", second[0], 0)
    groups = (
        (x, mixed, run, size, grad_scan, total),
        (grad_end, start),
        (kernel_rows, bias_full, skip_wide),
        (masks, seg_col, seg_row, writers, readers, turned),
    )
    last_args = (states, kernel_state, bias_state_row, grad_read)
    back = run_back(True, *groups, last_args, ())
    back, out_grad, gate_grad = lax.optimization_barrier((back, out_grad, gate_grad))
    grad_mixed, sums, grad_states, state_sums, rate, direct = back
    for a, b in zip(first[1:], second[1:]):
        out_grad = halve(out_grad, "seq", a, 0)
        gate_grad = halve(gate_grad, "seq", b, 0)
    edges = jnp.concatenate([grad_mixed[HALO - 8 : HALO], grad_states[HALO - 8 : HALO]], axis=1)
    edges = chunk_permute(edges, rows, lambda c: c - 1)
    edges, out_grad, gate_grad = lax.optimization_barrier((edges, out_grad, gate_grad))
    early = split_blocks(jnp.stack([out_grad, gate_grad]), local_inner)
    none = early[0][:0]
    for b in range(bits_of(head_devices)):
        early, none = sum_blocks_step(early, none, b)
    early = early[0]
    fill = ((length - 8, 0), (0, 0))
    grad_values_in = (grad_mixed[HALO:] + jnp.pad(edges[:, :inner], fill)).astype(BF16)
    grad_states_in = (grad_states[HALO:] + jnp.pad(edges[:, inner:], fill)).astype(BF16)

    kept = jnp.stack([sums[6].reshape(-1, LANES).sum(1), sums[7].reshape(-1, LANES).sum(1)], axis=1)
    rate_end = sums[5].reshape(heads, HEADDIM).sum(1) + passing * kept.reshape(heads)
    grad_log_decay = rate[:, :heads] + rate_end
    grad_step_size = direct[:, :heads] - grad_log_decay * decay_full
    grad_step_raw = grad_step_size * jax.nn.sigmoid(step_raw)
    grad_step_in = grad_step_raw.astype(BF16)
    grad_decay_log = jnp.sum(grad_log_decay * log_decay, axis=0)
    grad_step_bias = jnp.sum(grad_step_raw, axis=0)
    grad_skip_gain = gate_sums[1].reshape(heads, HEADDIM).sum(1)

    grad_normed = (
        grad_normed
        + dot_turned(grad_values_in, value_full)
        + dot_turned(grad_states_in, state_weight)
        + dot_turned(grad_step_in, step_full)
    )
    grad_norm_gain = jnp.sum(grad_normed * hidden * norm_scale, axis=0)
    grad_unit = grad_normed * norm_gain
    change = norm_scale * grad_unit - hidden * norm_scale**3 * jnp.mean(
        grad_unit * hidden, axis=1, keepdims=True
    )
    change, early = lax.optimization_barrier((change.astype(BF16), early))
    changes = lax.all_gather(change, "head").reshape(rows, block, width)
    input_gradient = cotangent.astype(F32) + changes.astype(F32)

    pieces = [
        grad_norm_gain,
        sums[:taps],
        state_sums[:taps],
        sums[4],
        state_sums[4],
        grad_step_bias,
        grad_decay_log,
        grad_skip_gain,
        gate_sums[0],
    ]
    flat = jnp.concatenate([piece.reshape(-1) for piece in pieces])
    lines = -(-flat.shape[0] // (8 * LANES)) * 8
    flat = jnp.pad(flat, (0, lines * LANES - flat.shape[0])).reshape(lines, LANES)
    tail = jnp.concatenate(
        [
            dot_rows(normed, grad_values_in).astype(BF16),
            dot_rows(normed, grad_states_in).astype(BF16),
            dot_rows(normed, pad_lanes(grad_step_in)).astype(BF16),
        ],
        axis=1,
    )
    tail = tail.reshape(2, width // 2, tail.shape[1])

    tail = halve(tail, "seq", 0, 1)
    flat = flat + swap(flat, "seq", 0)
    upper, lower = tail[0], tail[1]
    for a, b in zip(first, second):
        upper, lower = halve(upper, "seq", a, 0), halve(lower, "seq", b, 0)
        flat = flat + swap(flat, "seq", a)
    tail = jnp.stack([upper, lower])
    part = tail.shape[1]
    blocks = split_blocks(tail[:, :, :inner], local_inner)
    shared = split_blocks(tail[:, :, inner:], local_inner)
    wide = shared.shape[0]
    shared = shared.reshape((-1,) + shared.shape[2:])
    for b in range(bits_of(head_devices)):
        blocks, shared = sum_blocks_step(blocks, shared, b)
        flat = flat + swap(flat, "head", b)
    blocks = blocks[0]
    late = (1 + wide) * local_inner
    sides = []
    for i in range(2):
        own_part = jnp.concatenate([blocks[i], *shared[i::2]], axis=1)
        other = jnp.concatenate([early[i, :part], early[i, part:]], axis=1)
        other = jnp.pad(other, ((0, 0), (0, late - other.shape[1])))
        sides.append(jnp.concatenate([own_part, other], axis=0)[None])
    upper, lower = sides
    for a, b in zip(reversed(first), reversed(second)):
        upper, lower = join_seq(upper, a, 0), join_seq(lower, b, 0)
    sides = join_seq(jnp.stack([upper, lower], axis=1), 0, 0).astype(F32)
    tail = sides[:, :, :part].transpose(1, 0, 2, 3).reshape(width, late)
    early = sides[:, :, part:, : 2 * local_inner].reshape(seq_count, 2, part, 2, local_inner)
    early = early.transpose(1, 0, 3, 2, 4).reshape(2, width, local_inner)
    grad_output_weight = early[0].T
    grad_gate_weight = early[1]
    grad_value_weight = tail[:, :local_inner]
    shared = tail[:, local_inner:]
    flat = flat.reshape(-1)
    summed, at = [], 0
    for piece in pieces:
        summed.append(flat[at : at + piece.size].reshape(piece.shape))
        at += piece.size
    summed = [shared[:, : 2 * STATE], shared[:, 2 * STATE : 2 * STATE + heads]] + summed

    def own(value, axis):
        size = value.shape[axis] // head_devices
        return lax.dynamic_slice_in_dim(value, head_index * size, size, axis)

    return (
        block_output,
        input_gradient,
        summed[2],
        grad_gate_weight,
        grad_value_weight,
        summed[0],
        own(summed[1], 1),
        own(summed[3], 1),
        summed[4],
        own(summed[5], 0),
        summed[6],
        own(summed[7], 0),
        own(summed[8], 0),
        own(summed[9], 0),
        own(summed[10], 0),
        grad_output_weight,
    )


def solution(mesh):
    placed = (
        P(None, "seq", None),
        P(),
        P(),
        P(None, "head"),
        P(None, "head"),
        P(),
        P(None, "head"),
        P(None, "head"),
        P(),
        P("head"),
        P(),
        P("head"),
        P("head"),
        P("head"),
        P("head"),
        P("head", None),
        P(None, "seq", None),
    )
    return jax.shard_map(
        shards,
        mesh=mesh,
        in_specs=placed,
        out_specs=(
            P(None, "seq", None),
            P(None, "seq", None),
            P(),
            P(None, "head"),
            P(None, "head"),
            P(),
            P(None, "head"),
            P(None, "head"),
            P(),
            P("head"),
            P(),
            P("head"),
            P("head"),
            P("head"),
            P("head"),
            P("head", None),
        ),
        check_vma=False,
    )
```

```python
import functools

import jax
import jax.numpy as jnp
from jax import lax
from jax.experimental import pallas as pl
from jax.experimental.pallas import tpu as pltpu
from jax.sharding import PartitionSpec as P

HEADDIM = 64
STATE = 128
EPSILON = 1e-05
HIGHEST = lax.Precision.HIGHEST
LANES = 128
HALO = 16
TILE = 256
BF16 = jnp.bfloat16
F32 = jnp.float32
VMEM_LIMIT = 56 * 1024 * 1024


def bits_of(count):
    return count.bit_length() - 1


def swap(value, axis, bit):
    count = lax.axis_size(axis)
    return lax.ppermute(value, axis, [(i, i ^ (1 << bit)) for i in range(count)])


def bit_of(axis, bit):
    return (lax.axis_index(axis) >> bit) & 1


def joined(mine, other, upper, axis):
    return jnp.where(
        upper == 1,
        jnp.concatenate([other, mine], axis=axis),
        jnp.concatenate([mine, other], axis=axis),
    )


def swap_orders():
    bits = bits_of(lax.axis_size("seq"))
    return list(range(1, bits)), list(reversed(range(1, bits)))


def seq_rank(order):
    return sum(bit_of("seq", b) << (len(order) - 1 - i) for i, b in enumerate(order))


def join_seq(value, bit, axis):
    return joined(value, swap(value, "seq", bit), bit_of("seq", bit), axis)


def gather_blocks(value):
    count, place = lax.axis_size("head"), lax.axis_index("head")
    got = [value]
    for d in range(1, count):
        got.append(lax.ppermute(value, "head", [(i, (i + d) % count) for i in range(count)]))
    blocks = []
    for h in range(count):
        block = value
        for d in range(1, count):
            block = jnp.where(place == (h + d) % count, got[d], block)
        blocks.append(block)
    return blocks


def three_parts(value):
    parts = []
    for _ in range(3):
        part = lax.reduce_precision(value, 8, 7)
        parts.append(part.astype(BF16))
        value = value - part
    return parts


def gather_columns(weight, extra):
    first, second = swap_orders()
    half, columns = weight.shape[0] // 2, weight.shape[1]
    part = half // lax.axis_size("seq")
    lines = -(-extra.shape[0] // (16 * columns)) * 16
    extra_rows = jnp.pad(extra, (0, lines * columns - extra.shape[0])).reshape(lines, columns)
    own = [
        lax.dynamic_slice_in_dim(weight, at + seq_rank([0] + order) * part, part, 0)
        for at, order in ((0, first), (half, second))
    ]
    blocks = gather_blocks(jnp.concatenate([*own, extra_rows], axis=0))
    whole = jnp.concatenate([block[: 2 * part] for block in blocks], axis=1)
    extras = jnp.stack([block[2 * part :].reshape(-1)[: extra.shape[0]] for block in blocks])
    upper, lower = whole[:part], whole[part:]
    for a, b in zip(reversed(first), reversed(second)):
        upper, lower = join_seq(upper, a, 0), join_seq(lower, b, 0)
    whole = join_seq(jnp.stack([upper, lower]), 0, 1)
    return whole.reshape(weight.shape[0], whole.shape[2]), extras


def halve(value, name, bit, axis):
    size = value.shape[axis] // 2
    upper = bit_of(name, bit)
    keep = lax.dynamic_slice_in_dim(value, upper * size, size, axis)
    send = lax.dynamic_slice_in_dim(value, (1 - upper) * size, size, axis)
    got = swap(send, name, bit)
    return (keep.astype(F32) + got.astype(F32)).astype(value.dtype)


def split_blocks(value, size):
    count = value.shape[-1] // size
    return jnp.stack([value[..., h * size : (h + 1) * size] for h in range(count)])


def sum_blocks_step(blocks, shared, bit):
    count = blocks.shape[0]
    pairs = blocks.reshape((count // 2, 2) + blocks.shape[1:])
    upper = bit_of("head", bit)
    keep = lax.dynamic_index_in_dim(pairs, upper, 1, keepdims=False)
    send = lax.dynamic_index_in_dim(pairs, 1 - upper, 1, keepdims=False)
    shape = keep.shape
    keep = jnp.concatenate([keep.reshape((-1,) + shape[2:]), shared], axis=0)
    send = jnp.concatenate([send.reshape((-1,) + shape[2:]), shared], axis=0)
    total = (keep.astype(F32) + swap(send, "head", bit).astype(F32)).astype(blocks.dtype)
    most = shape[0] * shape[1]
    return total[:most].reshape(shape), total[most:]


def chunk_permute(value, rows, target):
    seq_count, head_count = lax.axis_size("seq"), lax.axis_size("head")
    parts = head_count // rows
    pairs = []
    for s in range(seq_count):
        for h in range(head_count):
            goal = target(s * parts + h % parts)
            if 0 <= goal < seq_count * parts:
                place = (goal // parts) * head_count + (h // parts) * parts + goal % parts
                pairs.append((s * head_count + h, place))
    return lax.ppermute(value, ("seq", "head"), pairs)


def carried(rate, state, rows, chunk, reverse, meanwhile):
    count = lax.axis_size("seq") * (lax.axis_size("head") // rows)
    levels = bits_of(count)
    size = state.shape[0] // 2
    heads = rate.shape[0]
    side = chunk & 1
    done = []

    def exchange(value, rate, level, step):
        coarse = lax.reduce_precision(rate, 8, 7)
        fine = (rate - coarse).astype(BF16)
        coarse = coarse.astype(BF16)
        tail = jnp.pad(jnp.stack([coarse, fine]), ((0, 14), (0, STATE - heads)))
        message = jnp.concatenate([value.astype(BF16), tail], axis=0)
        if step < len(meanwhile) and meanwhile[step] is not None:
            work, operands, ordered = meanwhile[step]
            if ordered:
                message, operands = lax.optimization_barrier((message, operands))
            got = chunk_permute(message, rows, lambda c: c ^ (1 << level))
            got, extra = lax.optimization_barrier((got, work(*operands)))
            done.append(extra)
        else:
            got = chunk_permute(message, rows, lambda c: c ^ (1 << level))
        pair = got[size : size + 2, :heads].astype(F32)
        return got[:size].astype(F32), pair[0] + pair[1]

    def widen(rate):
        return lax.dynamic_slice_in_dim(jnp.repeat(rate, HEADDIM), side * size, size, 0)[:, None]

    low = state.astype(BF16)
    send = lax.dynamic_slice_in_dim(low, (1 - side) * size, size, 0)
    mine = lax.dynamic_slice_in_dim(state, side * size, size, 0)
    theirs, their_rate = exchange(send, rate, 0, 0)
    comes_second = side == (0 if reverse else 1)
    earlier = jnp.where(comes_second, theirs, mine)
    later = jnp.where(comes_second, mine, theirs)
    first_rate = jnp.where(comes_second, their_rate, rate)
    second_rate = jnp.where(comes_second, rate, their_rate)
    total = widen(second_rate) * earlier + later
    total_rate = rate * their_rate
    before = jnp.zeros_like(total)
    before_rate = jnp.ones_like(rate)
    for b in range(1, levels):
        got, got_rate = exchange(total, total_rate, b, b)
        after = ((chunk >> b) & 1) == (0 if reverse else 1)
        before = jnp.where(after, widen(before_rate) * got + before, before)
        before_rate = jnp.where(after, before_rate * got_rate, before_rate)
        if b < levels - 1:
            total = jnp.where(
                after, widen(total_rate) * got + total, widen(got_rate) * total + got
            )
            total_rate = total_rate * got_rate
    second = widen(first_rate) * before + earlier
    own = jnp.where(comes_second, second, before).astype(BF16)
    other = jnp.where(comes_second, before, second).astype(BF16)
    got = chunk_permute(other, rows, lambda c: c ^ 1)
    return joined(own, got, side, 0), done


def contract(a, b, dims):
    return lax.dot_general(a, b, ((dims[0], dims[1]), ((), ())), preferred_element_type=F32)


def taps_of(padded, masks):
    taps = []
    for k in range(4):
        moved = padded if k == 3 else pltpu.roll(padded, 3 - k, 0)
        tap = moved[HALO:]
        taps.append(tap if k == 3 else tap * masks[:, k : k + 1])
    return taps


def summed_of(taps, kernel, bias):
    summed = bias
    for k in range(4):
        summed = summed + kernel[k : k + 1, :] * taps[k]
    return summed


def linked_of(seg_col, seg_row):
    length = seg_col.shape[0]
    row = lax.broadcasted_iota(jnp.int32, (length, length), 0)
    col = lax.broadcasted_iota(jnp.int32, (length, length), 1)
    return jnp.where((row >= col) & (seg_col == seg_row), 1.0, 0.0)


def blocks_of(length):
    count = length // TILE
    return [(t, s) for t in range(count) for s in range(t + 1)]


def cut(index):
    return slice(index * TILE, (index + 1) * TILE)


def scan_kernel(
    mixed_ref,
    states_ref,
    kernel_ref,
    bias_ref,
    kernel_state_ref,
    bias_state_ref,
    masks_ref,
    seg_col_ref,
    seg_row_ref,
    step_ref,
    decay_ref,
    x_ref,
    open_ref,
    end_ref,
    run_ref,
    size_ref,
    writers_ref,
    readers_ref,
    turned_ref,
    scores,
    run_all,
    size_all,
):
    pair = pl.program_id(0)
    length = x_ref.shape[0]
    pairs = run_all.shape[0]
    low = lax.broadcasted_iota(jnp.int32, (1, LANES), 1) < HEADDIM
    masks = masks_ref[...]

    @pl.when(pair == 0)
    def _():
        taps = taps_of(states_ref[...].astype(F32), masks)
        summed = summed_of(taps, kernel_state_ref[...], bias_state_ref[...])
        active = (summed * jax.nn.sigmoid(summed)).astype(BF16)
        writers = active[:, :STATE]
        readers = active[:, STATE:]
        writers_ref[...] = writers
        readers_ref[...] = readers
        linked = linked_of(seg_col_ref[...], seg_row_ref[...])
        scores[...] = contract(readers, writers, ((1,), (1,))) * linked
        row = lax.broadcasted_iota(jnp.int32, (length, length), 0)
        col = lax.broadcasted_iota(jnp.int32, (length, length), 1)
        lower = jnp.where(row >= col, 1.0, 0.0)
        run = jnp.dot(lower, decay_ref[...], precision=HIGHEST, preferred_element_type=F32)
        turned_ref[...] = run.T
        size = step_ref[...]
        for i in range(pairs):
            a, b = 2 * i, 2 * i + 1
            run_all[i] = jnp.where(low, run[:, a : a + 1], run[:, b : b + 1])
            size_all[i] = jnp.where(low, size[:, a : a + 1], size[:, b : b + 1])

    run = run_all[pair]
    size = size_all[pair]
    run_ref[...] = run
    size_ref[...] = size
    taps = taps_of(mixed_ref[...].astype(F32), masks)
    summed = summed_of(taps, kernel_ref[...], bias_ref[...])
    x = (summed * jax.nn.sigmoid(summed)).astype(BF16)
    x_ref[...] = x
    sized = x.astype(F32) * size
    sized_low = sized.astype(BF16)
    zero = jnp.zeros((), BF16)
    halves = (jnp.where(low, sized_low, zero), jnp.where(low, zero, sized_low))
    totals = [None] * (length // TILE)
    for t, s in blocks_of(length):
        score = scores[cut(t), cut(s)]
        for j in range(2):
            row = turned_ref[pl.ds(2 * pair + j, 1), :][:, cut(s)]
            col = run[cut(t), j * HEADDIM : j * HEADDIM + 1]
            weight = (score * jnp.exp(jnp.minimum(col - row, 0.0))).astype(BF16)
            part = contract(weight, halves[j][cut(s)], ((1,), (0,)))
            totals[t] = part if totals[t] is None else totals[t] + part
    for t, total in enumerate(totals):
        open_ref[cut(t), :] = total
    seg_col = seg_col_ref[...]
    last = jnp.where(seg_col == seg_col[length - 1 : length, :], 1.0, 0.0)
    toward = last * jnp.exp(run[length - 1 : length, :] - run)
    end_ref[...] = contract((toward * sized).astype(BF16), writers_ref[...], ((0,), (0,)))


def gate_kernel(
    open_ref,
    x_ref,
    run_ref,
    gate_ref,
    grad_out_ref,
    hidden_ref,
    entered_ref,
    readers_ref,
    start_ref,
    weight_ref,
    gain_ref,
    skip_ref,
    total_ref,
    out_in_ref,
    block_ref,
    grad_scan_ref,
    grad_gate_ref,
    grad_read_ref,
    sums_ref,
    grad_start_ref,
):
    step = pl.program_id(0)
    inner = gain_ref.shape[1]
    gain = gain_ref[...]
    x = x_ref[...].astype(F32)
    start = start_ref[...]
    readers = readers_ref[...]
    reach = entered_ref[...] * jnp.exp(run_ref[...])
    total = open_ref[...] + reach * contract(readers, start, ((1,), (1,)))
    total_ref[...] = total
    scanned = total + skip_ref[...] * x
    gate = gate_ref[...]
    sig = jax.nn.sigmoid(gate)
    act = gate * sig
    gated = scanned * act
    scale = lax.rsqrt(jnp.sum(gated * gated, axis=1, keepdims=True) / inner + EPSILON)
    unit = gated * scale
    out_in = (unit * gain).astype(BF16)
    out_in_ref[...] = out_in
    branch = contract(out_in, weight_ref[...], ((1,), (1,)))
    block_ref[...] = (hidden_ref[...].astype(F32) + branch).astype(BF16)
    grad_out = grad_out_ref[...]
    q = grad_out * gain
    inner_product = jnp.sum(q * gated, axis=1, keepdims=True) / inner
    grad_gated = scale * q - gated * (scale * scale * scale * inner_product)
    grad_scan = grad_gated * act
    grad_scan_low = grad_scan.astype(BF16)
    grad_scan_ref[...] = grad_scan_low
    slope = sig * (1.0 + gate * (1.0 - sig))
    grad_gate_ref[...] = (grad_gated * scanned * slope).astype(BF16)
    reached = (reach * grad_scan).astype(BF16)
    grad_read_ref[...] = contract(reached, start, ((1,), (0,)))
    grad_start = contract(reached, readers, ((0,), (0,)))
    gain_sum = jnp.sum(grad_out * unit, axis=0, keepdims=True)
    skip_sum = jnp.sum(grad_scan * x, axis=0, keepdims=True)
    rows = lax.broadcasted_iota(jnp.int32, (8, inner), 0)
    sums = jnp.where(rows == 0, gain_sum, jnp.where(rows == 1, skip_sum, 0.0))

    @pl.when(step == 0)
    def _():
        sums_ref[...] = sums
        grad_start_ref[...] = grad_start

    @pl.when(step > 0)
    def _():
        sums_ref[...] += sums
        grad_start_ref[...] += grad_start


def conv_back(grad_act, padded, kernel, bias, masks):
    length, width = grad_act.shape
    taps = taps_of(padded, masks)
    summed = summed_of(taps, kernel, bias)
    sig = jax.nn.sigmoid(summed)
    grad_u = grad_act * (sig * (1.0 + summed * (1.0 - sig)))
    rows = lax.broadcasted_iota(jnp.int32, (8, width), 0)
    sums = jnp.where(rows == 4, jnp.sum(grad_u, axis=0, keepdims=True), 0.0)
    mixed = None
    nothing = jnp.zeros((HALO, width), F32)
    for k in range(4):
        sums = jnp.where(rows == k, jnp.sum(grad_u * taps[k], axis=0, keepdims=True), sums)
        back = grad_u * kernel[k : k + 1, :]
        if k < 3:
            back = back * masks[:, k : k + 1]
        back = jnp.concatenate([nothing, back], axis=0)
        if k < 3:
            back = pltpu.roll(back, length + HALO - (3 - k), 0)
        mixed = back if mixed is None else mixed + back
    return mixed, sums


def back_kernel(
    x_ref,
    mixed_ref,
    run_ref,
    size_ref,
    grad_scan_ref,
    total_ref,
    grad_end_ref,
    start_ref,
    kernel_ref,
    bias_ref,
    skip_ref,
    masks_ref,
    seg_col_ref,
    seg_row_ref,
    writers_ref,
    readers_ref,
    turned_ref,
    states_ref,
    kernel_state_ref,
    bias_state_ref,
    grad_read_ref,
    raw_ref,
    decay_ref,
    rows_ref,
    grad_mixed_ref,
    ends_ref,
    sums_ref,
    grad_states_ref,
    ends_state_ref,
    sums_state_ref,
    grad_step_ref,
    sums_step_ref,
    scores,
    grad_scores,
    grad_write,
    rate_sum,
    direct_sum,
    end_sum,
):
    pair = pl.program_id(0)
    length = x_ref.shape[0]
    low = lax.broadcasted_iota(jnp.int32, (1, LANES), 1) < HEADDIM
    lane = lax.broadcasted_iota(jnp.int32, (1, LANES), 1)
    masks = masks_ref[...]
    writers = writers_ref[...]
    readers = readers_ref[...]
    seg_col = seg_col_ref[...]

    @pl.when(pair == 0)
    def _():
        linked = linked_of(seg_col, seg_row_ref[...])
        scores[...] = contract(readers, writers, ((1,), (1,))) * linked
        for total in (grad_scores, grad_write, rate_sum, direct_sum, end_sum):
            total[...] = jnp.zeros_like(total)

    run = run_ref[...]
    size = size_ref[...]
    x = x_ref[...].astype(F32)
    sized = x * size
    sized_low = sized.astype(BF16)
    grad_scan = grad_scan_ref[...]
    zero = jnp.zeros((), BF16)
    halves = (jnp.where(low, grad_scan, zero), jnp.where(low, zero, grad_scan))
    inner = [None] * (length // TILE)
    for t, s in blocks_of(length):
        score = scores[cut(t), cut(s)]
        grad_score = grad_scores[cut(t), cut(s)]
        for j in range(2):
            row = turned_ref[pl.ds(2 * pair + j, 1), :][:, cut(s)]
            col = run[cut(t), j * HEADDIM : j * HEADDIM + 1]
            decay = jnp.exp(jnp.minimum(col - row, 0.0))
            weight = (score * decay).astype(BF16)
            grad_weight = contract(halves[j][cut(t)], sized_low[cut(s)], ((1,), (1,)))
            grad_score = grad_score + grad_weight * decay
            part = contract(weight, halves[j][cut(t)], ((0,), (0,)))
            inner[s] = part if inner[s] is None else inner[s] + part
        grad_scores[cut(t), cut(s)] = grad_score
    inner = inner[0] if len(inner) == 1 else jnp.concatenate(inner, axis=0)
    final = jnp.where(seg_col == seg_col[length - 1 : length, :], 1.0, 0.0)
    toward = final * jnp.exp(run[length - 1 : length, :] - run)
    grad_end = grad_end_ref[...]
    outer = toward * contract(writers, grad_end.astype(BF16), ((1,), (1,)))
    grad_write[...] += contract(
        (toward * sized).astype(BF16), grad_end.astype(BF16), ((1,), (0,))
    )
    grad_sized = inner + outer
    grad_scan = grad_scan.astype(F32)
    sized_low = sized_low.astype(F32)
    change = grad_scan * total_ref[...] - sized_low * grad_sized
    straight = x * grad_sized
    for j in range(2):
        side = low if j == 0 else jnp.logical_not(low)
        here = lane == 2 * pair + j
        one = jnp.sum(jnp.where(side, change, 0.0), axis=1, keepdims=True)
        rate_sum[...] += jnp.where(here, one, 0.0)
        two = jnp.sum(jnp.where(side, straight, 0.0), axis=1, keepdims=True)
        direct_sum[...] += jnp.where(here, two, 0.0)
    grad_x = size * grad_sized + skip_ref[...] * grad_scan
    grad_mixed, sums = conv_back(
        grad_x, mixed_ref[...].astype(F32), kernel_ref[...], bias_ref[...], masks
    )
    grad_mixed_ref[...] = grad_mixed[HALO:].astype(BF16)
    ends_ref[...] = jnp.concatenate([grad_mixed[HALO - 8 : HALO], grad_mixed[length + HALO - 8 :]])
    sums_ref[...] = sums
    outer_sum = jnp.sum(sized_low * outer, axis=0, keepdims=True)
    kept = start_ref[...].astype(F32) * grad_end.astype(F32)
    keep = rows_ref[0:1, :]
    for j in range(2):
        side = low if j == 0 else jnp.logical_not(low)
        held = jnp.sum(kept[j * HEADDIM : (j + 1) * HEADDIM], keepdims=True)
        left = jnp.sum(jnp.where(side, outer_sum, 0.0), axis=1, keepdims=True)
        end_sum[...] += jnp.where(lane == 2 * pair + j, left + keep * held, 0.0)

    @pl.when(pair == pl.num_programs(0) - 1)
    def _():
        linked = linked_of(seg_col, seg_row_ref[...])
        grad_score = (grad_scores[...] * linked).astype(BF16)
        grad_readers = contract(grad_score, writers, ((1,), (0,))) + grad_read_ref[...]
        grad_writers = contract(grad_score, readers, ((0,), (0,))) + grad_write[...]
        grad_act = jnp.concatenate([grad_writers, grad_readers], axis=1)
        grad_states, state_sums = conv_back(
            grad_act,
            states_ref[...].astype(F32),
            kernel_state_ref[...],
            bias_state_ref[...],
            masks,
        )
        grad_states_ref[...] = grad_states[HALO:].astype(BF16)
        ends_state_ref[...] = jnp.concatenate(
            [grad_states[HALO - 8 : HALO], grad_states[length + HALO - 8 :]]
        )
        sums_state_ref[...] = state_sums
        row = lax.broadcasted_iota(jnp.int32, (length, length), 0)
        col = lax.broadcasted_iota(jnp.int32, (length, length), 1)
        upper = jnp.where(col >= row, 1.0, 0.0)
        grad_decay = end_sum[...] + jnp.dot(
            upper, rate_sum[...], precision=HIGHEST, preferred_element_type=F32
        )
        grad_raw = (direct_sum[...] - grad_decay * rows_ref[1:2, :]) * jax.nn.sigmoid(raw_ref[...])
        grad_step_ref[...] = grad_raw.astype(BF16)
        line = lax.broadcasted_iota(jnp.int32, (8, LANES), 0)
        decay_total = jnp.sum(grad_decay * decay_ref[...], axis=0, keepdims=True)
        raw_total = jnp.sum(grad_raw, axis=0, keepdims=True)
        sums_step_ref[...] = jnp.where(line == 0, decay_total, jnp.where(line == 1, raw_total, 0.0))


def input_kernel(
    mixed_ref,
    states_ref,
    step_ref,
    fix_ref,
    gate_ref,
    hidden_ref,
    scale_ref,
    gain_ref,
    value_ref,
    state_ref,
    step_weight_ref,
    gate_weight_ref,
    all_ref,
    change_ref,
    gain_sum_ref,
):
    step = pl.program_id(0)
    tile = mixed_ref.shape[0]
    both = jnp.concatenate([mixed_ref[...], states_ref[...]], axis=1)
    fix = fix_ref[...].astype(BF16)
    fixed = jnp.concatenate([jnp.zeros((tile - 16, fix.shape[1]), BF16), fix], axis=0)
    row = lax.broadcasted_iota(jnp.int32, (tile, 1), 0)
    last = (row >= tile - 8) & (step == pl.num_programs(0) - 1)
    both = jnp.where(last, fixed, both)
    inner = mixed_ref.shape[1]
    all_ref[...] = jnp.concatenate([both, step_ref[...]], axis=1)
    grad = contract(gate_ref[...], gate_weight_ref[...], ((1,), (1,)))
    grad = grad + contract(both[:, :inner], value_ref[...], ((1,), (1,)))
    grad = grad + contract(both[:, inner:], state_ref[...], ((1,), (1,)))
    grad = grad + contract(step_ref[...], step_weight_ref[...], ((1,), (1,)))
    hidden = hidden_ref[...].astype(F32)
    scale = scale_ref[...]
    grad_unit = grad * gain_ref[...]
    mean = jnp.sum(grad_unit * hidden, axis=1, keepdims=True) / hidden.shape[1]
    change_ref[...] = (scale * grad_unit - hidden * (scale * scale * scale * mean)).astype(BF16)
    gain_sum = jnp.sum(grad * hidden * scale, axis=0, keepdims=True)

    @pl.when(step == 0)
    def _():
        gain_sum_ref[...] = gain_sum

    @pl.when(step > 0)
    def _():
        gain_sum_ref[...] += gain_sum


def whole_spec(shape):
    return pl.BlockSpec(shape, lambda i: (0,) * len(shape))


def columns_spec(rows):
    return pl.BlockSpec((rows, LANES), lambda i: (0, i))


def rows_spec(rows, width):
    return pl.BlockSpec((rows, width), lambda i: (i, 0))


def run_scan(mixed, states, kernel, bias, kernel_state, bias_state, masks, seg_col, seg_row, step, decay):
    length = mixed.shape[0] - HALO
    inner = mixed.shape[1]
    pairs = inner // LANES
    wide = 2 * STATE
    return pl.pallas_call(
        scan_kernel,
        grid=(pairs,),
        in_specs=[
            columns_spec(length + HALO),
            whole_spec((length + HALO, wide)),
            columns_spec(4),
            columns_spec(1),
            whole_spec((4, wide)),
            whole_spec((1, wide)),
            whole_spec((length, 4)),
            whole_spec((length, 1)),
            whole_spec((1, length)),
            whole_spec((length, LANES)),
            whole_spec((length, LANES)),
        ],
        out_specs=[
            columns_spec(length),
            columns_spec(length),
            rows_spec(LANES, STATE),
            columns_spec(length),
            columns_spec(length),
            whole_spec((length, STATE)),
            whole_spec((length, STATE)),
            whole_spec((LANES, length)),
        ],
        out_shape=[
            jax.ShapeDtypeStruct((length, inner), BF16),
            jax.ShapeDtypeStruct((length, inner), F32),
            jax.ShapeDtypeStruct((inner, STATE), F32),
            jax.ShapeDtypeStruct((length, inner), F32),
            jax.ShapeDtypeStruct((length, inner), F32),
            jax.ShapeDtypeStruct((length, STATE), BF16),
            jax.ShapeDtypeStruct((length, STATE), BF16),
            jax.ShapeDtypeStruct((LANES, length), F32),
        ],
        scratch_shapes=[
            pltpu.VMEM((length, length), F32),
            pltpu.VMEM((pairs, length, LANES), F32),
            pltpu.VMEM((pairs, length, LANES), F32),
        ],
        compiler_params=pltpu.CompilerParams(vmem_limit_bytes=VMEM_LIMIT),
        name="scan_forward",
    )(mixed, states, kernel, bias, kernel_state, bias_state, masks, seg_col, seg_row, step, decay)


def run_gate(opened, x, run, gate, grad_out, hidden, entered, readers, start, weight, gain, skip):
    length, inner = x.shape
    width = hidden.shape[1]
    tile = 128
    return pl.pallas_call(
        gate_kernel,
        grid=(length // tile,),
        in_specs=[
            rows_spec(tile, inner),
            rows_spec(tile, inner),
            rows_spec(tile, inner),
            rows_spec(tile, inner),
            rows_spec(tile, inner),
            rows_spec(tile, width),
            rows_spec(tile, 1),
            rows_spec(tile, STATE),
            whole_spec((inner, STATE)),
            whole_spec((width, inner)),
            whole_spec((1, inner)),
            whole_spec((1, inner)),
        ],
        out_specs=[
            rows_spec(tile, inner),
            rows_spec(tile, inner),
            rows_spec(tile, width),
            rows_spec(tile, inner),
            rows_spec(tile, inner),
            rows_spec(tile, STATE),
            whole_spec((8, inner)),
            whole_spec((inner, STATE)),
        ],
        out_shape=[
            jax.ShapeDtypeStruct((length, inner), F32),
            jax.ShapeDtypeStruct((length, inner), BF16),
            jax.ShapeDtypeStruct((length, width), BF16),
            jax.ShapeDtypeStruct((length, inner), BF16),
            jax.ShapeDtypeStruct((length, inner), BF16),
            jax.ShapeDtypeStruct((length, STATE), F32),
            jax.ShapeDtypeStruct((8, inner), F32),
            jax.ShapeDtypeStruct((inner, STATE), F32),
        ],
        compiler_params=pltpu.CompilerParams(vmem_limit_bytes=VMEM_LIMIT),
        name="gate_both",
    )(opened, x, run, gate, grad_out, hidden, entered, readers, start, weight, gain, skip)


def run_back(wide_args, rows_args, row_args, whole_args):
    x = wide_args[0]
    length, inner = x.shape
    wide = 2 * STATE
    out = [
        ((length, inner), BF16),
        ((16, inner), F32),
        ((8, inner), F32),
        ((length, wide), BF16),
        ((16, wide), F32),
        ((8, wide), F32),
        ((length, LANES), BF16),
        ((8, LANES), F32),
    ]
    return pl.pallas_call(
        back_kernel,
        grid=(inner // LANES,),
        in_specs=[columns_spec(a.shape[0]) for a in wide_args]
        + [rows_spec(LANES, STATE) for a in rows_args]
        + [columns_spec(a.shape[0]) for a in row_args]
        + [whole_spec(a.shape) for a in whole_args],
        out_specs=[columns_spec(shape[0]) for shape, _ in out[:3]]
        + [whole_spec(shape) for shape, _ in out[3:]],
        out_shape=[jax.ShapeDtypeStruct(shape, kind) for shape, kind in out],
        scratch_shapes=[
            pltpu.VMEM((length, length), F32),
            pltpu.VMEM((length, length), F32),
            pltpu.VMEM((length, STATE), F32),
            pltpu.VMEM((length, LANES), F32),
            pltpu.VMEM((length, LANES), F32),
            pltpu.VMEM((1, LANES), F32),
        ],
        compiler_params=pltpu.CompilerParams(vmem_limit_bytes=VMEM_LIMIT),
        name="scan_backward",
    )(*wide_args, *rows_args, *row_args, *whole_args)


def run_input(mixed, states, step, fix, gate, hidden, scale, gain, weights):
    length, inner = mixed.shape
    width = hidden.shape[1]
    columns = inner + states.shape[1] + LANES
    tile = TILE
    return pl.pallas_call(
        input_kernel,
        grid=(length // tile,),
        in_specs=[
            rows_spec(tile, inner),
            rows_spec(tile, states.shape[1]),
            rows_spec(tile, LANES),
            whole_spec(fix.shape),
            rows_spec(tile, inner),
            rows_spec(tile, width),
            rows_spec(tile, 1),
            whole_spec((1, width)),
            *[whole_spec(weight.shape) for weight in weights],
        ],
        out_specs=[rows_spec(tile, columns), rows_spec(tile, width), whole_spec((1, width))],
        out_shape=[
            jax.ShapeDtypeStruct((length, columns), BF16),
            jax.ShapeDtypeStruct((length, width), BF16),
            jax.ShapeDtypeStruct((1, width), F32),
        ],
        compiler_params=pltpu.CompilerParams(vmem_limit_bytes=VMEM_LIMIT),
        name="input_gradient",
    )(mixed, states, step, fix, gate, hidden, scale, gain, *weights)


def dot(a, b):
    return jnp.dot(a, b, preferred_element_type=F32)


def dot_rows(a, b):
    return lax.dot_general(a, b, (((0,), (0,)), ((), ())), preferred_element_type=F32)


def dot_turned(a, b):
    return lax.dot_general(a, b, (((1,), (1,)), ((), ())), preferred_element_type=F32)


def pad_lanes(value):
    return jnp.pad(value, ((0, 0), (0, LANES - value.shape[1])))


def shards(
    hidden_states,
    segment_ids,
    norm_gain,
    gate_weight,
    value_weight,
    state_weight,
    step_weight,
    kernel_value,
    kernel_state,
    bias_value,
    bias_state,
    step_bias,
    decay_log,
    skip_gain,
    inner_gain,
    output_weight,
    cotangent,
):
    rows, block, width = hidden_states.shape
    head_devices = lax.axis_size("head")
    parts = head_devices // rows
    length = block // parts
    seq_index, head_index = lax.axis_index("seq"), lax.axis_index("head")
    row_index, part_index = head_index // parts, head_index % parts
    chunk = seq_index * parts + part_index
    local_inner = gate_weight.shape[1]
    local_heads = step_bias.shape[0]
    inner = local_inner * head_devices
    heads = local_heads * head_devices
    taps = kernel_value.shape[0]

    small = jnp.concatenate(
        [kernel_value.reshape(-1), bias_value, inner_gain, step_bias, decay_log, skip_gain]
    )
    count = small.shape[0]
    seq_count = lax.axis_size("seq")
    part = width // seq_count
    packed = jnp.concatenate(
        [
            lax.dynamic_slice_in_dim(weight, seq_index * part, part, 0)
            for weight in (gate_weight, output_weight.T)
        ],
        axis=0,
    )
    value_full, extras = gather_columns(
        value_weight, jnp.concatenate([*three_parts(small), step_weight.reshape(-1)])
    )
    small = sum(extras[:, i * count : (i + 1) * count].astype(F32) for i in range(3))
    step_full = extras[:, 3 * count :].reshape(head_devices, width, local_heads)
    step_full = step_full.transpose(1, 0, 2).reshape(width, heads)
    place = (row_index, part_index * length, 0)
    hidden_low = lax.dynamic_slice(hidden_states, place, (1, length, width))[0]
    packed, hidden_low = lax.optimization_barrier((packed, hidden_low))
    packed = lax.all_gather(packed, ("seq", "head"))
    packed = packed.reshape(seq_count, head_devices, 2 * part, local_inner)
    at = taps * local_inner
    kernel_full = small[:, :at].reshape(head_devices, taps, local_inner)
    kernel_full = kernel_full.transpose(1, 0, 2).reshape(taps, inner)
    bias_full = small[:, at : at + local_inner].reshape(1, inner)
    at += local_inner
    gain_full = small[:, at : at + local_inner].reshape(1, inner)
    at += local_inner
    step_bias_full = small[:, at : at + local_heads].reshape(heads)
    at += local_heads
    decay_full = jnp.exp(small[:, at : at + local_heads].reshape(heads))
    at += local_heads
    skip_full = small[:, at : at + local_heads].reshape(heads)
    skip_wide = jnp.repeat(skip_full, HEADDIM)[None]

    cot = lax.dynamic_slice(cotangent, place, (1, length, width))[0]
    edge = chunk_permute(hidden_low[length - HALO :], rows, lambda c: c + 1)
    hidden_ext = jnp.concatenate([edge, hidden_low], axis=0).astype(F32)
    scale_ext = lax.rsqrt(jnp.mean(hidden_ext * hidden_ext, axis=1, keepdims=True) + EPSILON)
    normed_ext = (hidden_ext * scale_ext * norm_gain).astype(BF16)
    normed = normed_ext[HALO:]
    hidden = hidden_low.astype(F32)
    norm_scale = scale_ext[HALO:]

    seg_line = lax.dynamic_slice_in_dim(segment_ids, row_index, 1, 0)[0]
    seg_line = jnp.concatenate([jnp.full((HALO,), -1, jnp.int32), seg_line])
    window = lax.dynamic_slice_in_dim(seg_line, chunk * length, length + HALO, 0)
    segments = window[HALO:]
    before = window[HALO - 1]
    masks = jnp.stack(
        [window[HALO - 3 + k : HALO - 3 + k + length] == segments for k in range(taps)], axis=1
    ).astype(F32)
    entered = (segments == before).astype(F32)[:, None]
    seg_col = segments.astype(F32)[:, None]
    seg_row = segments.astype(F32)[None]

    mixed = dot(normed_ext, value_full).astype(BF16)
    states = dot(normed_ext, state_weight).astype(BF16)
    step_wide = pad_lanes(step_full)
    decay_row = jnp.pad(decay_full, (0, LANES - heads))
    step_raw = dot(normed, step_wide) + jnp.pad(step_bias_full, (0, LANES - heads))
    step_size = jax.nn.softplus(step_raw)
    log_decay = -step_size * decay_row
    passing_row = jnp.exp(jnp.sum(log_decay, axis=0)) * (segments[length - 1] == before).astype(F32)
    passing = passing_row[:heads]

    kernel_rows = kernel_full
    bias_state_row = bias_state[None]
    x, opened, end_state, run, size, writers, readers, turned = run_scan(
        mixed,
        states,
        kernel_rows,
        bias_full,
        kernel_state,
        bias_state_row,
        masks,
        seg_col,
        seg_row,
        step_size,
        log_decay,
    )
    def make_gate(packed, normed):
        gate_full = packed[:, :, :part].transpose(0, 2, 1, 3).reshape(width, inner)
        return gate_full, dot(normed, gate_full)

    def make_out(packed, cot):
        output_full = packed[:, :, part:].transpose(0, 2, 1, 3).reshape(width, inner)
        return output_full, dot(cot, output_full)

    start, done = carried(
        passing,
        end_state,
        rows,
        chunk,
        False,
        (None, (make_gate, (packed, normed), False), (make_out, (packed, cot), False)),
    )
    gate_full, gate_pre = done[0]
    output_full, grad_out_in = done[1]
    total, out_in, block_rows, grad_scan, grad_gate, grad_read, gate_sums, grad_start = run_gate(
        opened,
        x,
        run,
        gate_pre,
        grad_out_in,
        hidden_low,
        entered,
        readers,
        start,
        output_full,
        gain_full,
        skip_wide,
    )
    block_output = lax.all_gather(block_rows, "head").reshape(rows, block, width)
    first, second = swap_orders()

    half = width // 2

    core = bit_of("seq", 0)

    def by_core(value):
        cut_up = value.reshape(length, 2, 2, half // 2)
        return tuple(
            lax.dynamic_index_in_dim(cut_up, side, 2, keepdims=False).reshape(length, half)
            for side in (core, 1 - core)
        )

    def core_sum(left, right):
        got = swap(dot_rows(left[1], right).astype(BF16), "seq", 0).astype(F32)
        return (dot_rows(left[0], right) + got).astype(BF16).reshape(2, half // 2, right.shape[1])

    def early_part(left, right):
        return dot_rows(left, right).astype(BF16).reshape(2, half, inner)

    grad_end, done = carried(
        passing,
        grad_start,
        rows,
        chunk,
        True,
        (
            None,
            (early_part, (cot, out_in), True),
            (early_part, (normed, grad_gate), True),
        ),
    )
    out_grad, gate_grad = (halve(part, "seq", 0, 1) for part in done)
    out_grad, gate_grad, grad_end = lax.optimization_barrier((out_grad, gate_grad, grad_end))
    out_grad = halve(out_grad, "seq", first[0], 1)
    gate_grad = halve(gate_grad, "seq", second[0], 1)
    step_rows = jnp.pad(jnp.stack([passing_row, decay_row]), ((0, 6), (0, 0)))
    back = run_back(
        (x, mixed, run, size, grad_scan, total),
        (grad_end, start),
        (kernel_rows, bias_full, skip_wide),
        (
            masks,
            seg_col,
            seg_row,
            writers,
            readers,
            turned,
            states,
            kernel_state,
            bias_state_row,
            grad_read,
            step_raw,
            log_decay,
            step_rows,
        ),
    )
    back, out_grad, gate_grad, block_output, normed = lax.optimization_barrier(
        (back, out_grad, gate_grad, block_output, normed)
    )
    normed_sides = by_core(normed)
    grad_mixed, ends, sums, grad_states, state_ends, state_sums, grad_step, step_sums = back
    ends = jnp.concatenate([ends, state_ends], axis=1)
    edges = chunk_permute(ends[:8], rows, lambda c: c - 1)
    edges, out_grad, gate_grad = lax.optimization_barrier((edges, out_grad, gate_grad))
    for a, b in zip(first[1:], second[1:]):
        out_grad = halve(out_grad, "seq", a, 1)
        gate_grad = halve(gate_grad, "seq", b, 1)
    fix = jnp.pad(ends[8:] + edges, ((8, 0), (0, 0)))
    everything, change, gain_sum = run_input(
        grad_mixed,
        grad_states,
        grad_step,
        fix,
        grad_gate,
        hidden_low,
        norm_scale,
        norm_gain[None],
        (value_full, state_weight, step_wide, gate_full),
    )
    grad_norm_gain = gain_sum[0]
    early = split_blocks(jnp.concatenate([out_grad, gate_grad], axis=0), local_inner)
    none = early[0][:0]
    early, everything = lax.optimization_barrier((early, everything))
    early, none = sum_blocks_step(early, none, 0)
    grad_decay_log, grad_step_bias = step_sums[0, :heads], step_sums[1, :heads]
    grad_skip_gain = gate_sums[1].reshape(heads, HEADDIM).sum(1)
    changes = lax.all_gather(change, "head").reshape(rows, block, width)

    pieces = [
        grad_norm_gain,
        sums[:taps],
        state_sums[:taps],
        sums[4],
        state_sums[4],
        grad_step_bias,
        grad_decay_log,
        grad_skip_gain,
        gate_sums[0],
    ]
    flat = jnp.concatenate([piece.reshape(-1) for piece in pieces])
    lines = -(-flat.shape[0] // (8 * LANES)) * 8
    flat = jnp.pad(flat, (0, lines * LANES - flat.shape[0])).reshape(lines, LANES)
    tail = core_sum(normed_sides, everything)
    tail, flat = lax.optimization_barrier((tail, flat))
    head_bits = bits_of(head_devices)
    order = [("head", b) for b in range(head_bits)] + [("seq", b) for b in first]
    upper, lower = tail[0], tail[1]
    flat = flat + swap(flat, "seq", 0)
    for a, b in zip(first, second):
        upper, lower = halve(upper, "seq", a, 0), halve(lower, "seq", b, 0)
        upper, lower, flat = lax.optimization_barrier((upper, lower, flat))
        flat = flat + swap(flat, *order.pop(0))
    tail = jnp.stack([upper, lower])
    part = tail.shape[1]
    blocks = split_blocks(tail[:, :, :inner], local_inner)
    shared = split_blocks(tail[:, :, inner:], local_inner)
    wide = shared.shape[0]
    shared = shared.reshape((-1,) + shared.shape[2:])
    for b in range(head_bits):
        if b > 0:
            early, none = sum_blocks_step(early, none, b)
        blocks, shared = sum_blocks_step(blocks, shared, b)
        if b < head_bits - 1:
            blocks, shared, early, flat = lax.optimization_barrier((blocks, shared, early, flat))
        flat = flat + swap(flat, *order.pop(0))
    early = early[0]
    blocks = blocks[0]
    flat = flat.reshape(-1)
    summed, at = [], 0
    for piece in pieces:
        summed.append(flat[at : at + piece.size].reshape(piece.shape))
        at += piece.size

    def own(value, axis):
        size = value.shape[axis] // head_devices
        return lax.dynamic_slice_in_dim(value, head_index * size, size, axis)

    for i, axis in ((1, 1), (3, 0), (5, 0), (6, 0), (7, 0), (8, 0)):
        summed[i] = own(summed[i], axis)
    sides = [
        jnp.concatenate([blocks[i], *shared[i::2], early[2 * i], early[2 * i + 1]], axis=1)
        for i in range(2)
    ]
    upper, lower = sides
    for a, b in zip(reversed(first), reversed(second)):
        upper, lower = join_seq(upper, a, 0), join_seq(lower, b, 0)
    input_gradient = cotangent.astype(F32) + changes.astype(F32)
    upper, lower, summed, input_gradient = lax.optimization_barrier(
        (upper, lower, summed, input_gradient)
    )
    sides = join_seq(jnp.stack([upper, lower]), 0, 1)
    late = (1 + wide) * local_inner

    def rows_of(side, at):
        return sides[side, :, at : at + local_inner].astype(F32)

    grad_output_weight = jnp.concatenate(
        [rows_of(0, late).T, rows_of(0, late + local_inner).T], axis=1
    )
    grad_gate_weight = jnp.concatenate([rows_of(1, late), rows_of(1, late + local_inner)], axis=0)
    grad_value_weight = jnp.concatenate([rows_of(0, 0), rows_of(1, 0)], axis=0)
    shared = sides[:, :, local_inner:late].reshape(width, late - local_inner).astype(F32)
    summed = [shared[:, : 2 * STATE], own(shared[:, 2 * STATE : 2 * STATE + heads], 1)] + summed

    return (
        block_output,
        input_gradient,
        summed[2],
        grad_gate_weight,
        grad_value_weight,
        summed[0],
        summed[1],
        *summed[3:],
        grad_output_weight,
    )


def solution(mesh):
    placed = (
        P(None, "seq", None),
        P(),
        P(),
        P(None, "head"),
        P(None, "head"),
        P(),
        P(None, "head"),
        P(None, "head"),
        P(),
        P("head"),
        P(),
        P("head"),
        P("head"),
        P("head"),
        P("head"),
        P("head", None),
        P(None, "seq", None),
    )
    return jax.shard_map(
        shards,
        mesh=mesh,
        in_specs=placed,
        out_specs=(
            P(None, "seq", None),
            P(None, "seq", None),
            P(),
            P(None, "head"),
            P(None, "head"),
            P(),
            P(None, "head"),
            P(None, "head"),
            P(),
            P("head"),
            P(),
            P("head"),
            P("head"),
            P("head"),
            P("head"),
            P("head", None),
        ),
        check_vma=False,
    )
```

```python
import functools

import jax
import jax.numpy as jnp
from jax import lax
from jax.experimental import pallas as pl
from jax.experimental.pallas import tpu as pltpu
from jax.sharding import PartitionSpec as P

HEADDIM = 64
STATE = 128
EPSILON = 1e-05
HIGHEST = lax.Precision.HIGHEST
LANES = 128
HALO = 16
TILE = 256
BF16 = jnp.bfloat16
F32 = jnp.float32
VMEM_LIMIT = 56 * 1024 * 1024


def bits_of(count):
    return count.bit_length() - 1


def swap(value, axis, bit):
    count = lax.axis_size(axis)
    return lax.ppermute(value, axis, [(i, i ^ (1 << bit)) for i in range(count)])


def bit_of(axis, bit):
    return (lax.axis_index(axis) >> bit) & 1


def joined(mine, other, upper, axis):
    return jnp.where(
        upper == 1,
        jnp.concatenate([other, mine], axis=axis),
        jnp.concatenate([mine, other], axis=axis),
    )


def swap_orders():
    bits = bits_of(lax.axis_size("seq"))
    return list(range(1, bits)), list(reversed(range(1, bits)))


def seq_rank(order):
    return sum(bit_of("seq", b) << (len(order) - 1 - i) for i, b in enumerate(order))


def join_seq(value, bit, axis):
    return joined(value, swap(value, "seq", bit), bit_of("seq", bit), axis)


def gather_blocks(value):
    count, place = lax.axis_size("head"), lax.axis_index("head")
    got = [value]
    for d in range(1, count):
        got.append(lax.ppermute(value, "head", [(i, (i + d) % count) for i in range(count)]))
    blocks = []
    for h in range(count):
        block = value
        for d in range(1, count):
            block = jnp.where(place == (h + d) % count, got[d], block)
        blocks.append(block)
    return blocks


def three_parts(value):
    parts = []
    for _ in range(3):
        part = lax.reduce_precision(value, 8, 7)
        parts.append(part.astype(BF16))
        value = value - part
    return parts


def gather_columns(weight, extra):
    first, second = swap_orders()
    half, columns = weight.shape[0] // 2, weight.shape[1]
    part = half // lax.axis_size("seq")
    lines = -(-extra.shape[0] // (16 * columns)) * 16
    extra_rows = jnp.pad(extra, (0, lines * columns - extra.shape[0])).reshape(lines, columns)
    own = [
        lax.dynamic_slice_in_dim(weight, at + seq_rank([0] + order) * part, part, 0)
        for at, order in ((0, first), (half, second))
    ]
    blocks = gather_blocks(jnp.concatenate([*own, extra_rows], axis=0))
    whole = jnp.concatenate([block[: 2 * part] for block in blocks], axis=1)
    extras = jnp.stack([block[2 * part :].reshape(-1)[: extra.shape[0]] for block in blocks])
    upper, lower = whole[:part], whole[part:]
    for a, b in zip(reversed(first), reversed(second)):
        upper, lower = join_seq(upper, a, 0), join_seq(lower, b, 0)
    whole = join_seq(jnp.stack([upper, lower]), 0, 1)
    return whole.reshape(weight.shape[0], whole.shape[2]), extras


def halve(value, name, bit, axis):
    size = value.shape[axis] // 2
    upper = bit_of(name, bit)
    keep = lax.dynamic_slice_in_dim(value, upper * size, size, axis)
    send = lax.dynamic_slice_in_dim(value, (1 - upper) * size, size, axis)
    got = swap(send, name, bit)
    return (keep.astype(F32) + got.astype(F32)).astype(value.dtype)


def split_blocks(value, size):
    count = value.shape[-1] // size
    return jnp.stack([value[..., h * size : (h + 1) * size] for h in range(count)])


def sum_blocks_step(blocks, shared, bit):
    count = blocks.shape[0]
    pairs = blocks.reshape((count // 2, 2) + blocks.shape[1:])
    upper = bit_of("head", bit)
    keep = lax.dynamic_index_in_dim(pairs, upper, 1, keepdims=False)
    send = lax.dynamic_index_in_dim(pairs, 1 - upper, 1, keepdims=False)
    shape = keep.shape
    keep = jnp.concatenate([keep.reshape((-1,) + shape[2:]), shared], axis=0)
    send = jnp.concatenate([send.reshape((-1,) + shape[2:]), shared], axis=0)
    total = (keep.astype(F32) + swap(send, "head", bit).astype(F32)).astype(blocks.dtype)
    most = shape[0] * shape[1]
    return total[:most].reshape(shape), total[most:]


def chunk_permute(value, rows, target):
    seq_count, head_count = lax.axis_size("seq"), lax.axis_size("head")
    parts = head_count // rows
    pairs = []
    for s in range(seq_count):
        for h in range(head_count):
            goal = target(s * parts + h % parts)
            if 0 <= goal < seq_count * parts:
                place = (goal // parts) * head_count + (h // parts) * parts + goal % parts
                pairs.append((s * head_count + h, place))
    return lax.ppermute(value, ("seq", "head"), pairs)


def carried(rate, state, rows, chunk, reverse, meanwhile):
    count = lax.axis_size("seq") * (lax.axis_size("head") // rows)
    levels = bits_of(count)
    size = state.shape[0] // 2
    heads = rate.shape[0]
    side = chunk & 1
    done = []

    def exchange(value, rate, level, step):
        coarse = lax.reduce_precision(rate, 8, 7)
        fine = (rate - coarse).astype(BF16)
        coarse = coarse.astype(BF16)
        tail = jnp.pad(jnp.stack([coarse, fine]), ((0, 14), (0, STATE - heads)))
        message = jnp.concatenate([value.astype(BF16), tail], axis=0)
        if step < len(meanwhile) and meanwhile[step] is not None:
            work, operands, ordered = meanwhile[step]
            if ordered:
                message, operands = lax.optimization_barrier((message, operands))
            got = chunk_permute(message, rows, lambda c: c ^ (1 << level))
            got, extra = lax.optimization_barrier((got, work(*operands)))
            done.append(extra)
        else:
            got = chunk_permute(message, rows, lambda c: c ^ (1 << level))
        pair = got[size : size + 2, :heads].astype(F32)
        return got[:size].astype(F32), pair[0] + pair[1]

    def widen(rate):
        return lax.dynamic_slice_in_dim(jnp.repeat(rate, HEADDIM), side * size, size, 0)[:, None]

    low = state.astype(BF16)
    send = lax.dynamic_slice_in_dim(low, (1 - side) * size, size, 0)
    mine = lax.dynamic_slice_in_dim(state, side * size, size, 0)
    theirs, their_rate = exchange(send, rate, 0, 0)
    comes_second = side == (0 if reverse else 1)
    earlier = jnp.where(comes_second, theirs, mine)
    later = jnp.where(comes_second, mine, theirs)
    first_rate = jnp.where(comes_second, their_rate, rate)
    second_rate = jnp.where(comes_second, rate, their_rate)
    total = widen(second_rate) * earlier + later
    total_rate = rate * their_rate
    before = jnp.zeros_like(total)
    before_rate = jnp.ones_like(rate)
    for b in range(1, levels):
        got, got_rate = exchange(total, total_rate, b, b)
        after = ((chunk >> b) & 1) == (0 if reverse else 1)
        before = jnp.where(after, widen(before_rate) * got + before, before)
        before_rate = jnp.where(after, before_rate * got_rate, before_rate)
        if b < levels - 1:
            total = jnp.where(
                after, widen(total_rate) * got + total, widen(got_rate) * total + got
            )
            total_rate = total_rate * got_rate
    second = widen(first_rate) * before + earlier
    own = jnp.where(comes_second, second, before).astype(BF16)
    other = jnp.where(comes_second, before, second).astype(BF16)
    got = chunk_permute(other, rows, lambda c: c ^ 1)
    return joined(own, got, side, 0), done


def contract(a, b, dims):
    return lax.dot_general(a, b, ((dims[0], dims[1]), ((), ())), preferred_element_type=F32)


def taps_of(padded, masks):
    taps = []
    for k in range(4):
        moved = padded if k == 3 else pltpu.roll(padded, 3 - k, 0)
        tap = moved[HALO:]
        taps.append(tap if k == 3 else tap * masks[:, k : k + 1])
    return taps


def summed_of(taps, kernel, bias):
    summed = bias
    for k in range(4):
        summed = summed + kernel[k : k + 1, :] * taps[k]
    return summed


def linked_of(seg_col, seg_row):
    length = seg_col.shape[0]
    row = lax.broadcasted_iota(jnp.int32, (length, length), 0)
    col = lax.broadcasted_iota(jnp.int32, (length, length), 1)
    return jnp.where((row >= col) & (seg_col == seg_row), 1.0, 0.0)


def blocks_of(length):
    count = length // TILE
    return [(t, s) for t in range(count) for s in range(t + 1)]


def cut(index):
    return slice(index * TILE, (index + 1) * TILE)


def scan_kernel(
    mixed_ref,
    states_ref,
    kernel_ref,
    bias_ref,
    kernel_state_ref,
    bias_state_ref,
    masks_ref,
    seg_col_ref,
    seg_row_ref,
    step_ref,
    decay_ref,
    x_ref,
    open_ref,
    end_ref,
    run_ref,
    size_ref,
    writers_ref,
    readers_ref,
    turned_ref,
    scores,
    run_all,
    size_all,
):
    pair = pl.program_id(0)
    length = x_ref.shape[0]
    pairs = run_all.shape[0]
    low = lax.broadcasted_iota(jnp.int32, (1, LANES), 1) < HEADDIM
    masks = masks_ref[...]

    @pl.when(pair == 0)
    def _():
        taps = taps_of(states_ref[...].astype(F32), masks)
        summed = summed_of(taps, kernel_state_ref[...], bias_state_ref[...])
        active = (summed * jax.nn.sigmoid(summed)).astype(BF16)
        writers = active[:, :STATE]
        readers = active[:, STATE:]
        writers_ref[...] = writers
        readers_ref[...] = readers
        linked = linked_of(seg_col_ref[...], seg_row_ref[...])
        scores[...] = contract(readers, writers, ((1,), (1,))) * linked
        row = lax.broadcasted_iota(jnp.int32, (length, length), 0)
        col = lax.broadcasted_iota(jnp.int32, (length, length), 1)
        lower = jnp.where(row >= col, 1.0, 0.0)
        run = jnp.dot(lower, decay_ref[...], precision=HIGHEST, preferred_element_type=F32)
        turned_ref[...] = run.T
        size = step_ref[...]
        for i in range(pairs):
            a, b = 2 * i, 2 * i + 1
            run_all[i] = jnp.where(low, run[:, a : a + 1], run[:, b : b + 1])
            size_all[i] = jnp.where(low, size[:, a : a + 1], size[:, b : b + 1])

    run = run_all[pair]
    size = size_all[pair]
    run_ref[...] = run
    size_ref[...] = size
    taps = taps_of(mixed_ref[...].astype(F32), masks)
    summed = summed_of(taps, kernel_ref[...], bias_ref[...])
    x = (summed * jax.nn.sigmoid(summed)).astype(BF16)
    x_ref[...] = x
    sized = x.astype(F32) * size
    sized_low = sized.astype(BF16)
    zero = jnp.zeros((), BF16)
    halves = (jnp.where(low, sized_low, zero), jnp.where(low, zero, sized_low))
    totals = [None] * (length // TILE)
    for t, s in blocks_of(length):
        score = scores[cut(t), cut(s)]
        for j in range(2):
            row = turned_ref[pl.ds(2 * pair + j, 1), :][:, cut(s)]
            col = run[cut(t), j * HEADDIM : j * HEADDIM + 1]
            weight = (score * jnp.exp(jnp.minimum(col - row, 0.0))).astype(BF16)
            part = contract(weight, halves[j][cut(s)], ((1,), (0,)))
            totals[t] = part if totals[t] is None else totals[t] + part
    for t, total in enumerate(totals):
        open_ref[cut(t), :] = total
    seg_col = seg_col_ref[...]
    last = jnp.where(seg_col == seg_col[length - 1 : length, :], 1.0, 0.0)
    toward = last * jnp.exp(run[length - 1 : length, :] - run)
    end_ref[...] = contract((toward * sized).astype(BF16), writers_ref[...], ((0,), (0,)))


def gate_kernel(
    open_ref,
    x_ref,
    run_ref,
    gate_ref,
    grad_out_ref,
    hidden_ref,
    entered_ref,
    readers_ref,
    start_ref,
    weight_ref,
    gain_ref,
    skip_ref,
    total_ref,
    out_in_ref,
    block_ref,
    grad_scan_ref,
    grad_gate_ref,
    grad_read_ref,
    sums_ref,
    grad_start_ref,
):
    step = pl.program_id(0)
    inner = gain_ref.shape[1]
    gain = gain_ref[...]
    x = x_ref[...].astype(F32)
    start = start_ref[...]
    readers = readers_ref[...]
    reach = entered_ref[...] * jnp.exp(run_ref[...])
    total = open_ref[...] + reach * contract(readers, start, ((1,), (1,)))
    total_ref[...] = total
    scanned = total + skip_ref[...] * x
    gate = gate_ref[...]
    sig = jax.nn.sigmoid(gate)
    act = gate * sig
    gated = scanned * act
    scale = lax.rsqrt(jnp.sum(gated * gated, axis=1, keepdims=True) / inner + EPSILON)
    unit = gated * scale
    out_in = (unit * gain).astype(BF16)
    out_in_ref[...] = out_in
    branch = contract(out_in, weight_ref[...], ((1,), (1,)))
    block_ref[...] = (hidden_ref[...].astype(F32) + branch).astype(BF16)
    grad_out = grad_out_ref[...]
    q = grad_out * gain
    inner_product = jnp.sum(q * gated, axis=1, keepdims=True) / inner
    grad_gated = scale * q - gated * (scale * scale * scale * inner_product)
    grad_scan = grad_gated * act
    grad_scan_low = grad_scan.astype(BF16)
    grad_scan_ref[...] = grad_scan_low
    slope = sig * (1.0 + gate * (1.0 - sig))
    grad_gate_ref[...] = (grad_gated * scanned * slope).astype(BF16)
    reached = (reach * grad_scan).astype(BF16)
    grad_read_ref[...] = contract(reached, start, ((1,), (0,)))
    grad_start = contract(reached, readers, ((0,), (0,)))
    gain_sum = jnp.sum(grad_out * unit, axis=0, keepdims=True)
    skip_sum = jnp.sum(grad_scan * x, axis=0, keepdims=True)
    rows = lax.broadcasted_iota(jnp.int32, (8, inner), 0)
    sums = jnp.where(rows == 0, gain_sum, jnp.where(rows == 1, skip_sum, 0.0))

    @pl.when(step == 0)
    def _():
        sums_ref[...] = sums
        grad_start_ref[...] = grad_start

    @pl.when(step > 0)
    def _():
        sums_ref[...] += sums
        grad_start_ref[...] += grad_start


def conv_back(grad_act, padded, kernel, bias, masks):
    length, width = grad_act.shape
    taps = taps_of(padded, masks)
    summed = summed_of(taps, kernel, bias)
    sig = jax.nn.sigmoid(summed)
    grad_u = grad_act * (sig * (1.0 + summed * (1.0 - sig)))
    rows = lax.broadcasted_iota(jnp.int32, (8, width), 0)
    sums = jnp.where(rows == 4, jnp.sum(grad_u, axis=0, keepdims=True), 0.0)
    mixed = None
    nothing = jnp.zeros((HALO, width), F32)
    for k in range(4):
        sums = jnp.where(rows == k, jnp.sum(grad_u * taps[k], axis=0, keepdims=True), sums)
        back = grad_u * kernel[k : k + 1, :]
        if k < 3:
            back = back * masks[:, k : k + 1]
        back = jnp.concatenate([nothing, back], axis=0)
        if k < 3:
            back = pltpu.roll(back, length + HALO - (3 - k), 0)
        mixed = back if mixed is None else mixed + back
    return mixed, sums


def back_kernel(
    x_ref,
    mixed_ref,
    run_ref,
    size_ref,
    grad_scan_ref,
    total_ref,
    grad_end_ref,
    start_ref,
    kernel_ref,
    bias_ref,
    skip_ref,
    masks_ref,
    seg_col_ref,
    seg_row_ref,
    writers_ref,
    readers_ref,
    turned_ref,
    states_ref,
    kernel_state_ref,
    bias_state_ref,
    grad_read_ref,
    raw_ref,
    decay_ref,
    rows_ref,
    grad_mixed_ref,
    ends_ref,
    sums_ref,
    grad_states_ref,
    ends_state_ref,
    sums_state_ref,
    grad_step_ref,
    sums_step_ref,
    scores,
    grad_scores,
    grad_write,
    rate_sum,
    direct_sum,
    end_sum,
):
    pair = pl.program_id(0)
    length = x_ref.shape[0]
    low = lax.broadcasted_iota(jnp.int32, (1, LANES), 1) < HEADDIM
    lane = lax.broadcasted_iota(jnp.int32, (1, LANES), 1)
    masks = masks_ref[...]
    writers = writers_ref[...]
    readers = readers_ref[...]
    seg_col = seg_col_ref[...]

    @pl.when(pair == 0)
    def _():
        linked = linked_of(seg_col, seg_row_ref[...])
        scores[...] = contract(readers, writers, ((1,), (1,))) * linked
        for total in (grad_scores, grad_write, rate_sum, direct_sum, end_sum):
            total[...] = jnp.zeros_like(total)

    run = run_ref[...]
    size = size_ref[...]
    x = x_ref[...].astype(F32)
    sized = x * size
    sized_low = sized.astype(BF16)
    grad_scan = grad_scan_ref[...]
    zero = jnp.zeros((), BF16)
    halves = (jnp.where(low, grad_scan, zero), jnp.where(low, zero, grad_scan))
    inner = [None] * (length // TILE)
    for t, s in blocks_of(length):
        score = scores[cut(t), cut(s)]
        grad_score = grad_scores[cut(t), cut(s)]
        for j in range(2):
            row = turned_ref[pl.ds(2 * pair + j, 1), :][:, cut(s)]
            col = run[cut(t), j * HEADDIM : j * HEADDIM + 1]
            decay = jnp.exp(jnp.minimum(col - row, 0.0))
            weight = (score * decay).astype(BF16)
            grad_weight = contract(halves[j][cut(t)], sized_low[cut(s)], ((1,), (1,)))
            grad_score = grad_score + grad_weight * decay
            part = contract(weight, halves[j][cut(t)], ((0,), (0,)))
            inner[s] = part if inner[s] is None else inner[s] + part
        grad_scores[cut(t), cut(s)] = grad_score
    inner = inner[0] if len(inner) == 1 else jnp.concatenate(inner, axis=0)
    final = jnp.where(seg_col == seg_col[length - 1 : length, :], 1.0, 0.0)
    toward = final * jnp.exp(run[length - 1 : length, :] - run)
    grad_end = grad_end_ref[...]
    outer = toward * contract(writers, grad_end.astype(BF16), ((1,), (1,)))
    grad_write[...] += contract(
        (toward * sized).astype(BF16), grad_end.astype(BF16), ((1,), (0,))
    )
    grad_sized = inner + outer
    grad_scan = grad_scan.astype(F32)
    sized_low = sized_low.astype(F32)
    change = grad_scan * total_ref[...] - sized_low * grad_sized
    straight = x * grad_sized
    for j in range(2):
        side = low if j == 0 else jnp.logical_not(low)
        here = lane == 2 * pair + j
        one = jnp.sum(jnp.where(side, change, 0.0), axis=1, keepdims=True)
        rate_sum[...] += jnp.where(here, one, 0.0)
        two = jnp.sum(jnp.where(side, straight, 0.0), axis=1, keepdims=True)
        direct_sum[...] += jnp.where(here, two, 0.0)
    grad_x = size * grad_sized + skip_ref[...] * grad_scan
    grad_mixed, sums = conv_back(
        grad_x, mixed_ref[...].astype(F32), kernel_ref[...], bias_ref[...], masks
    )
    grad_mixed_ref[...] = grad_mixed[HALO:].astype(BF16)
    ends_ref[...] = jnp.concatenate([grad_mixed[HALO - 8 : HALO], grad_mixed[length + HALO - 8 :]])
    sums_ref[...] = sums
    outer_sum = jnp.sum(sized_low * outer, axis=0, keepdims=True)
    kept = start_ref[...].astype(F32) * grad_end.astype(F32)
    keep = rows_ref[0:1, :]
    for j in range(2):
        side = low if j == 0 else jnp.logical_not(low)
        held = jnp.sum(kept[j * HEADDIM : (j + 1) * HEADDIM], keepdims=True)
        left = jnp.sum(jnp.where(side, outer_sum, 0.0), axis=1, keepdims=True)
        end_sum[...] += jnp.where(lane == 2 * pair + j, left + keep * held, 0.0)

    @pl.when(pair == pl.num_programs(0) - 1)
    def _():
        linked = linked_of(seg_col, seg_row_ref[...])
        grad_score = (grad_scores[...] * linked).astype(BF16)
        grad_readers = contract(grad_score, writers, ((1,), (0,))) + grad_read_ref[...]
        grad_writers = contract(grad_score, readers, ((0,), (0,))) + grad_write[...]
        grad_act = jnp.concatenate([grad_writers, grad_readers], axis=1)
        grad_states, state_sums = conv_back(
            grad_act,
            states_ref[...].astype(F32),
            kernel_state_ref[...],
            bias_state_ref[...],
            masks,
        )
        grad_states_ref[...] = grad_states[HALO:].astype(BF16)
        ends_state_ref[...] = jnp.concatenate(
            [grad_states[HALO - 8 : HALO], grad_states[length + HALO - 8 :]]
        )
        sums_state_ref[...] = state_sums
        row = lax.broadcasted_iota(jnp.int32, (length, length), 0)
        col = lax.broadcasted_iota(jnp.int32, (length, length), 1)
        upper = jnp.where(col >= row, 1.0, 0.0)
        grad_decay = end_sum[...] + jnp.dot(
            upper, rate_sum[...], precision=HIGHEST, preferred_element_type=F32
        )
        grad_raw = (direct_sum[...] - grad_decay * rows_ref[1:2, :]) * jax.nn.sigmoid(raw_ref[...])
        grad_step_ref[...] = grad_raw.astype(BF16)
        line = lax.broadcasted_iota(jnp.int32, (8, LANES), 0)
        decay_total = jnp.sum(grad_decay * decay_ref[...], axis=0, keepdims=True)
        raw_total = jnp.sum(grad_raw, axis=0, keepdims=True)
        sums_step_ref[...] = jnp.where(line == 0, decay_total, jnp.where(line == 1, raw_total, 0.0))


def input_kernel(
    mixed_ref,
    states_ref,
    step_ref,
    fix_ref,
    gate_ref,
    hidden_ref,
    scale_ref,
    gain_ref,
    value_ref,
    state_ref,
    step_weight_ref,
    gate_weight_ref,
    all_ref,
    change_ref,
    gain_sum_ref,
):
    step = pl.program_id(0)
    tile = mixed_ref.shape[0]
    both = jnp.concatenate([mixed_ref[...], states_ref[...]], axis=1)
    fix = fix_ref[...].astype(BF16)
    fixed = jnp.concatenate([jnp.zeros((tile - 16, fix.shape[1]), BF16), fix], axis=0)
    row = lax.broadcasted_iota(jnp.int32, (tile, 1), 0)
    last = (row >= tile - 8) & (step == pl.num_programs(0) - 1)
    both = jnp.where(last, fixed, both)
    inner = mixed_ref.shape[1]
    all_ref[...] = jnp.concatenate([both, step_ref[...]], axis=1)
    grad = contract(gate_ref[...], gate_weight_ref[...], ((1,), (1,)))
    grad = grad + contract(both[:, :inner], value_ref[...], ((1,), (1,)))
    grad = grad + contract(both[:, inner:], state_ref[...], ((1,), (1,)))
    grad = grad + contract(step_ref[...], step_weight_ref[...], ((1,), (1,)))
    hidden = hidden_ref[...].astype(F32)
    scale = scale_ref[...]
    grad_unit = grad * gain_ref[...]
    mean = jnp.sum(grad_unit * hidden, axis=1, keepdims=True) / hidden.shape[1]
    change_ref[...] = (scale * grad_unit - hidden * (scale * scale * scale * mean)).astype(BF16)
    gain_sum = jnp.sum(grad * hidden * scale, axis=0, keepdims=True)

    @pl.when(step == 0)
    def _():
        gain_sum_ref[...] = gain_sum

    @pl.when(step > 0)
    def _():
        gain_sum_ref[...] += gain_sum


def whole_spec(shape):
    return pl.BlockSpec(shape, lambda i: (0,) * len(shape))


def columns_spec(rows):
    return pl.BlockSpec((rows, LANES), lambda i: (0, i))


def rows_spec(rows, width):
    return pl.BlockSpec((rows, width), lambda i: (i, 0))


def run_scan(mixed, states, kernel, bias, kernel_state, bias_state, masks, seg_col, seg_row, step, decay):
    length = mixed.shape[0] - HALO
    inner = mixed.shape[1]
    pairs = inner // LANES
    wide = 2 * STATE
    return pl.pallas_call(
        scan_kernel,
        grid=(pairs,),
        in_specs=[
            columns_spec(length + HALO),
            whole_spec((length + HALO, wide)),
            columns_spec(4),
            columns_spec(1),
            whole_spec((4, wide)),
            whole_spec((1, wide)),
            whole_spec((length, 4)),
            whole_spec((length, 1)),
            whole_spec((1, length)),
            whole_spec((length, LANES)),
            whole_spec((length, LANES)),
        ],
        out_specs=[
            columns_spec(length),
            columns_spec(length),
            rows_spec(LANES, STATE),
            columns_spec(length),
            columns_spec(length),
            whole_spec((length, STATE)),
            whole_spec((length, STATE)),
            whole_spec((LANES, length)),
        ],
        out_shape=[
            jax.ShapeDtypeStruct((length, inner), BF16),
            jax.ShapeDtypeStruct((length, inner), F32),
            jax.ShapeDtypeStruct((inner, STATE), F32),
            jax.ShapeDtypeStruct((length, inner), F32),
            jax.ShapeDtypeStruct((length, inner), F32),
            jax.ShapeDtypeStruct((length, STATE), BF16),
            jax.ShapeDtypeStruct((length, STATE), BF16),
            jax.ShapeDtypeStruct((LANES, length), F32),
        ],
        scratch_shapes=[
            pltpu.VMEM((length, length), F32),
            pltpu.VMEM((pairs, length, LANES), F32),
            pltpu.VMEM((pairs, length, LANES), F32),
        ],
        compiler_params=pltpu.CompilerParams(vmem_limit_bytes=VMEM_LIMIT),
        name="scan_forward",
    )(mixed, states, kernel, bias, kernel_state, bias_state, masks, seg_col, seg_row, step, decay)


def run_gate(opened, x, run, gate, grad_out, hidden, entered, readers, start, weight, gain, skip):
    length, inner = x.shape
    width = hidden.shape[1]
    tile = TILE
    return pl.pallas_call(
        gate_kernel,
        grid=(length // tile,),
        in_specs=[
            rows_spec(tile, inner),
            rows_spec(tile, inner),
            rows_spec(tile, inner),
            rows_spec(tile, inner),
            rows_spec(tile, inner),
            rows_spec(tile, width),
            rows_spec(tile, 1),
            rows_spec(tile, STATE),
            whole_spec((inner, STATE)),
            whole_spec((width, inner)),
            whole_spec((1, inner)),
            whole_spec((1, inner)),
        ],
        out_specs=[
            rows_spec(tile, inner),
            rows_spec(tile, inner),
            rows_spec(tile, width),
            rows_spec(tile, inner),
            rows_spec(tile, inner),
            rows_spec(tile, STATE),
            whole_spec((8, inner)),
            whole_spec((inner, STATE)),
        ],
        out_shape=[
            jax.ShapeDtypeStruct((length, inner), F32),
            jax.ShapeDtypeStruct((length, inner), BF16),
            jax.ShapeDtypeStruct((length, width), BF16),
            jax.ShapeDtypeStruct((length, inner), BF16),
            jax.ShapeDtypeStruct((length, inner), BF16),
            jax.ShapeDtypeStruct((length, STATE), F32),
            jax.ShapeDtypeStruct((8, inner), F32),
            jax.ShapeDtypeStruct((inner, STATE), F32),
        ],
        compiler_params=pltpu.CompilerParams(vmem_limit_bytes=VMEM_LIMIT),
        name="gate_both",
    )(opened, x, run, gate, grad_out, hidden, entered, readers, start, weight, gain, skip)


def run_back(wide_args, rows_args, row_args, whole_args):
    x = wide_args[0]
    length, inner = x.shape
    wide = 2 * STATE
    out = [
        ((length, inner), BF16),
        ((16, inner), F32),
        ((8, inner), F32),
        ((length, wide), BF16),
        ((16, wide), F32),
        ((8, wide), F32),
        ((length, LANES), BF16),
        ((8, LANES), F32),
    ]
    return pl.pallas_call(
        back_kernel,
        grid=(inner // LANES,),
        in_specs=[columns_spec(a.shape[0]) for a in wide_args]
        + [rows_spec(LANES, STATE) for a in rows_args]
        + [columns_spec(a.shape[0]) for a in row_args]
        + [whole_spec(a.shape) for a in whole_args],
        out_specs=[columns_spec(shape[0]) for shape, _ in out[:3]]
        + [whole_spec(shape) for shape, _ in out[3:]],
        out_shape=[jax.ShapeDtypeStruct(shape, kind) for shape, kind in out],
        scratch_shapes=[
            pltpu.VMEM((length, length), F32),
            pltpu.VMEM((length, length), F32),
            pltpu.VMEM((length, STATE), F32),
            pltpu.VMEM((length, LANES), F32),
            pltpu.VMEM((length, LANES), F32),
            pltpu.VMEM((1, LANES), F32),
        ],
        compiler_params=pltpu.CompilerParams(vmem_limit_bytes=VMEM_LIMIT),
        name="scan_backward",
    )(*wide_args, *rows_args, *row_args, *whole_args)


def run_input(mixed, states, step, fix, gate, hidden, scale, gain, weights):
    length, inner = mixed.shape
    width = hidden.shape[1]
    columns = inner + states.shape[1] + LANES
    tile = TILE
    return pl.pallas_call(
        input_kernel,
        grid=(length // tile,),
        in_specs=[
            rows_spec(tile, inner),
            rows_spec(tile, states.shape[1]),
            rows_spec(tile, LANES),
            whole_spec(fix.shape),
            rows_spec(tile, inner),
            rows_spec(tile, width),
            rows_spec(tile, 1),
            whole_spec((1, width)),
            *[whole_spec(weight.shape) for weight in weights],
        ],
        out_specs=[rows_spec(tile, columns), rows_spec(tile, width), whole_spec((1, width))],
        out_shape=[
            jax.ShapeDtypeStruct((length, columns), BF16),
            jax.ShapeDtypeStruct((length, width), BF16),
            jax.ShapeDtypeStruct((1, width), F32),
        ],
        compiler_params=pltpu.CompilerParams(vmem_limit_bytes=VMEM_LIMIT),
        name="input_gradient",
    )(mixed, states, step, fix, gate, hidden, scale, gain, *weights)


def dot(a, b):
    return jnp.dot(a, b, preferred_element_type=F32)


def dot_rows(a, b):
    return lax.dot_general(a, b, (((0,), (0,)), ((), ())), preferred_element_type=F32)


def dot_turned(a, b):
    return lax.dot_general(a, b, (((1,), (1,)), ((), ())), preferred_element_type=F32)


def pad_lanes(value):
    return jnp.pad(value, ((0, 0), (0, LANES - value.shape[1])))


def shards(
    hidden_states,
    segment_ids,
    norm_gain,
    gate_weight,
    value_weight,
    state_weight,
    step_weight,
    kernel_value,
    kernel_state,
    bias_value,
    bias_state,
    step_bias,
    decay_log,
    skip_gain,
    inner_gain,
    output_weight,
    cotangent,
):
    rows, block, width = hidden_states.shape
    head_devices = lax.axis_size("head")
    parts = head_devices // rows
    length = block // parts
    seq_index, head_index = lax.axis_index("seq"), lax.axis_index("head")
    row_index, part_index = head_index // parts, head_index % parts
    chunk = seq_index * parts + part_index
    local_inner = gate_weight.shape[1]
    local_heads = step_bias.shape[0]
    inner = local_inner * head_devices
    heads = local_heads * head_devices
    taps = kernel_value.shape[0]

    small = jnp.concatenate(
        [kernel_value.reshape(-1), bias_value, inner_gain, step_bias, decay_log, skip_gain]
    )
    count = small.shape[0]
    seq_count = lax.axis_size("seq")
    part = width // seq_count
    packed = jnp.concatenate(
        [
            lax.dynamic_slice_in_dim(weight, seq_index * part, part, 0)
            for weight in (gate_weight, output_weight.T)
        ],
        axis=0,
    )
    value_full, extras = gather_columns(
        value_weight, jnp.concatenate([*three_parts(small), step_weight.reshape(-1)])
    )
    small = sum(extras[:, i * count : (i + 1) * count].astype(F32) for i in range(3))
    step_full = extras[:, 3 * count :].reshape(head_devices, width, local_heads)
    step_full = step_full.transpose(1, 0, 2).reshape(width, heads)
    place = (row_index, part_index * length, 0)
    hidden_low = lax.dynamic_slice(hidden_states, place, (1, length, width))[0]
    packed, hidden_low = lax.optimization_barrier((packed, hidden_low))
    packed = lax.all_gather(packed, ("seq", "head"))
    packed = packed.reshape(seq_count, head_devices, 2 * part, local_inner)
    at = taps * local_inner
    kernel_full = small[:, :at].reshape(head_devices, taps, local_inner)
    kernel_full = kernel_full.transpose(1, 0, 2).reshape(taps, inner)
    bias_full = small[:, at : at + local_inner].reshape(1, inner)
    at += local_inner
    gain_full = small[:, at : at + local_inner].reshape(1, inner)
    at += local_inner
    step_bias_full = small[:, at : at + local_heads].reshape(heads)
    at += local_heads
    decay_full = jnp.exp(small[:, at : at + local_heads].reshape(heads))
    at += local_heads
    skip_full = small[:, at : at + local_heads].reshape(heads)
    skip_wide = jnp.repeat(skip_full, HEADDIM)[None]

    cot = lax.dynamic_slice(cotangent, place, (1, length, width))[0]
    edge = chunk_permute(hidden_low[length - HALO :], rows, lambda c: c + 1)
    hidden_ext = jnp.concatenate([edge, hidden_low], axis=0).astype(F32)
    scale_ext = lax.rsqrt(jnp.mean(hidden_ext * hidden_ext, axis=1, keepdims=True) + EPSILON)
    normed_ext = (hidden_ext * scale_ext * norm_gain).astype(BF16)
    normed = normed_ext[HALO:]
    hidden = hidden_low.astype(F32)
    norm_scale = scale_ext[HALO:]

    seg_line = lax.dynamic_slice_in_dim(segment_ids, row_index, 1, 0)[0]
    seg_line = jnp.concatenate([jnp.full((HALO,), -1, jnp.int32), seg_line])
    window = lax.dynamic_slice_in_dim(seg_line, chunk * length, length + HALO, 0)
    segments = window[HALO:]
    before = window[HALO - 1]
    masks = jnp.stack(
        [window[HALO - 3 + k : HALO - 3 + k + length] == segments for k in range(taps)], axis=1
    ).astype(F32)
    entered = (segments == before).astype(F32)[:, None]
    seg_col = segments.astype(F32)[:, None]
    seg_row = segments.astype(F32)[None]

    mixed = dot(normed_ext, value_full).astype(BF16)
    states = dot(normed_ext, state_weight).astype(BF16)
    states, cot = lax.optimization_barrier((states, cot))
    step_wide = pad_lanes(step_full)
    decay_row = jnp.pad(decay_full, (0, LANES - heads))
    step_raw = dot(normed, step_wide) + jnp.pad(step_bias_full, (0, LANES - heads))
    step_size = jax.nn.softplus(step_raw)
    log_decay = -step_size * decay_row
    passing_row = jnp.exp(jnp.sum(log_decay, axis=0)) * (segments[length - 1] == before).astype(F32)
    passing = passing_row[:heads]

    kernel_rows = kernel_full
    bias_state_row = bias_state[None]
    x, opened, end_state, run, size, writers, readers, turned = run_scan(
        mixed,
        states,
        kernel_rows,
        bias_full,
        kernel_state,
        bias_state_row,
        masks,
        seg_col,
        seg_row,
        step_size,
        log_decay,
    )
    def make_gate(packed, normed):
        gate_full = packed[:, :, :part].transpose(0, 2, 1, 3).reshape(width, inner)
        return gate_full, dot(normed, gate_full)

    def make_out(packed, cot):
        output_full = packed[:, :, part:].transpose(0, 2, 1, 3).reshape(width, inner)
        return output_full, dot(cot, output_full)

    start, done = carried(
        passing,
        end_state,
        rows,
        chunk,
        False,
        (None, (make_gate, (packed, normed), False), (make_out, (packed, cot), False)),
    )
    gate_full, gate_pre = done[0]
    output_full, grad_out_in = done[1]
    total, out_in, block_rows, grad_scan, grad_gate, grad_read, gate_sums, grad_start = run_gate(
        opened,
        x,
        run,
        gate_pre,
        grad_out_in,
        hidden_low,
        entered,
        readers,
        start,
        output_full,
        gain_full,
        skip_wide,
    )
    block_output = lax.all_gather(block_rows, "head").reshape(rows, block, width)
    first, second = swap_orders()

    half = width // 2

    core = bit_of("seq", 0)

    def by_core(value):
        cut_up = value.reshape(length, 2, 2, half // 2)
        return tuple(
            lax.dynamic_index_in_dim(cut_up, side, 2, keepdims=False).reshape(length, half)
            for side in (core, 1 - core)
        )

    def core_sum(left, right):
        got = swap(dot_rows(left[1], right).astype(BF16), "seq", 0).astype(F32)
        return (dot_rows(left[0], right) + got).astype(BF16).reshape(2, half // 2, right.shape[1])

    def early_part(left, right):
        return dot_rows(left, right).astype(BF16).reshape(2, half, inner)

    grad_end, done = carried(
        passing,
        grad_start,
        rows,
        chunk,
        True,
        (
            None,
            (early_part, (cot, out_in), True),
            (early_part, (normed, grad_gate), True),
        ),
    )
    out_grad, gate_grad = (halve(part, "seq", 0, 1) for part in done)
    out_grad, gate_grad, grad_end = lax.optimization_barrier((out_grad, gate_grad, grad_end))
    out_grad = halve(out_grad, "seq", first[0], 1)
    gate_grad = halve(gate_grad, "seq", second[0], 1)
    step_rows = jnp.pad(jnp.stack([passing_row, decay_row]), ((0, 6), (0, 0)))
    back = run_back(
        (x, mixed, run, size, grad_scan, total),
        (grad_end, start),
        (kernel_rows, bias_full, skip_wide),
        (
            masks,
            seg_col,
            seg_row,
            writers,
            readers,
            turned,
            states,
            kernel_state,
            bias_state_row,
            grad_read,
            step_raw,
            log_decay,
            step_rows,
        ),
    )
    back, out_grad, gate_grad, block_output, normed = lax.optimization_barrier(
        (back, out_grad, gate_grad, block_output, normed)
    )
    normed_sides = by_core(normed)
    grad_mixed, ends, sums, grad_states, state_ends, state_sums, grad_step, step_sums = back
    ends = jnp.concatenate([ends, state_ends], axis=1)
    edges = chunk_permute(ends[:8], rows, lambda c: c - 1)
    edges, out_grad, gate_grad = lax.optimization_barrier((edges, out_grad, gate_grad))
    for a, b in zip(first[1:], second[1:]):
        out_grad = halve(out_grad, "seq", a, 1)
        gate_grad = halve(gate_grad, "seq", b, 1)
    fix = jnp.pad(ends[8:] + edges, ((8, 0), (0, 0)))
    everything, change, gain_sum = run_input(
        grad_mixed,
        grad_states,
        grad_step,
        fix,
        grad_gate,
        hidden_low,
        norm_scale,
        norm_gain[None],
        (value_full, state_weight, step_wide, gate_full),
    )
    grad_norm_gain = gain_sum[0]
    early = split_blocks(jnp.concatenate([out_grad, gate_grad], axis=0), local_inner)
    none = early[0][:0]
    early, everything = lax.optimization_barrier((early, everything))
    early, none = sum_blocks_step(early, none, 0)
    grad_decay_log, grad_step_bias = step_sums[0, :heads], step_sums[1, :heads]
    grad_skip_gain = gate_sums[1].reshape(heads, HEADDIM).sum(1)
    changes = lax.all_gather(change, "head").reshape(rows, block, width)

    pieces = [
        grad_norm_gain,
        sums[:taps],
        state_sums[:taps],
        sums[4],
        state_sums[4],
        grad_step_bias,
        grad_decay_log,
        grad_skip_gain,
        gate_sums[0],
    ]
    flat = jnp.concatenate([piece.reshape(-1) for piece in pieces])
    lines = -(-flat.shape[0] // (8 * LANES)) * 8
    flat = jnp.pad(flat, (0, lines * LANES - flat.shape[0])).reshape(lines, LANES)
    tail = core_sum(normed_sides, everything)
    tail, flat = lax.optimization_barrier((tail, flat))
    head_bits = bits_of(head_devices)
    order = [("head", b) for b in range(head_bits)] + [("seq", b) for b in first]
    upper, lower = tail[0], tail[1]
    flat = flat + swap(flat, "seq", 0)
    for a, b in zip(first, second):
        upper, lower = halve(upper, "seq", a, 0), halve(lower, "seq", b, 0)
        upper, lower, flat = lax.optimization_barrier((upper, lower, flat))
        flat = flat + swap(flat, *order.pop(0))
    tail = jnp.stack([upper, lower])
    part = tail.shape[1]
    blocks = split_blocks(tail[:, :, :inner], local_inner)
    shared = split_blocks(tail[:, :, inner:], local_inner)
    wide = shared.shape[0]
    shared = shared.reshape((-1,) + shared.shape[2:])
    for b in range(head_bits):
        if b > 0:
            early, none = sum_blocks_step(early, none, b)
        blocks, shared = sum_blocks_step(blocks, shared, b)
        if b < head_bits - 1:
            blocks, shared, early, flat = lax.optimization_barrier((blocks, shared, early, flat))
        flat = flat + swap(flat, *order.pop(0))
    early = early[0]
    blocks = blocks[0]
    flat = flat.reshape(-1)
    summed, at = [], 0
    for piece in pieces:
        summed.append(flat[at : at + piece.size].reshape(piece.shape))
        at += piece.size

    def own(value, axis):
        size = value.shape[axis] // head_devices
        return lax.dynamic_slice_in_dim(value, head_index * size, size, axis)

    for i, axis in ((1, 1), (3, 0), (5, 0), (6, 0), (7, 0), (8, 0)):
        summed[i] = own(summed[i], axis)
    sides = [
        jnp.concatenate([blocks[i], *shared[i::2], early[2 * i], early[2 * i + 1]], axis=1)
        for i in range(2)
    ]
    upper, lower = sides
    for a, b in zip(reversed(first), reversed(second)):
        upper, lower = join_seq(upper, a, 0), join_seq(lower, b, 0)
    input_gradient = cotangent.astype(F32) + changes.astype(F32)
    upper, lower, summed, input_gradient = lax.optimization_barrier(
        (upper, lower, summed, input_gradient)
    )
    sides = join_seq(jnp.stack([upper, lower]), 0, 1)
    late = (1 + wide) * local_inner

    def rows_of(side, at):
        return sides[side, :, at : at + local_inner].astype(F32)

    grad_output_weight = jnp.concatenate(
        [rows_of(0, late).T, rows_of(0, late + local_inner).T], axis=1
    )
    grad_gate_weight = jnp.concatenate([rows_of(1, late), rows_of(1, late + local_inner)], axis=0)
    grad_value_weight = jnp.concatenate([rows_of(0, 0), rows_of(1, 0)], axis=0)
    shared = sides[:, :, local_inner:late].reshape(width, late - local_inner).astype(F32)
    summed = [shared[:, : 2 * STATE], own(shared[:, 2 * STATE : 2 * STATE + heads], 1)] + summed

    return (
        block_output,
        input_gradient,
        summed[2],
        grad_gate_weight,
        grad_value_weight,
        summed[0],
        summed[1],
        *summed[3:],
        grad_output_weight,
    )


def solution(mesh):
    placed = (
        P(None, "seq", None),
        P(),
        P(),
        P(None, "head"),
        P(None, "head"),
        P(),
        P(None, "head"),
        P(None, "head"),
        P(),
        P("head"),
        P(),
        P("head"),
        P("head"),
        P("head"),
        P("head"),
        P("head", None),
        P(None, "seq", None),
    )
    return jax.shard_map(
        shards,
        mesh=mesh,
        in_specs=placed,
        out_specs=(
            P(None, "seq", None),
            P(None, "seq", None),
            P(),
            P(None, "head"),
            P(None, "head"),
            P(),
            P(None, "head"),
            P(None, "head"),
            P(),
            P("head"),
            P(),
            P("head"),
            P("head"),
            P("head"),
            P("head"),
            P("head", None),
        ),
        check_vma=False,
    )
```
